32 devices in a mesh: dp: 4 (over z), expert: 8 (over y, x, core).
Axes of the slice: x: 2, y: 2, z: 4, core: 2. Of those that a mesh axis runs over, the one named last changes fastest.
Arguments:
- attn_input: bfloat16 [4096, 3072], P(('dp', 'expert')), may hold values from -6 to 6
- key_cot: bfloat16 [4096, 512], P(('dp', 'expert')), may hold values from -6 to 6
- routing: int32 [4096, 4], P(('dp', 'expert')), may hold values from 0 to 7, all different within a row; in each aligned block of 128 rows (0 to 127, 128 to 255, ...) at most 66 rows name the same one
- router_base: float32 [4096, 8], P(('dp', 'expert')), may hold values from -1.5 to 1.5
- router_weight: bfloat16 [3072, 8], replicated, may hold values from -2 to 2
- expert_rows: bfloat16 [256, 66, 3072], P(('dp', 'expert')), may hold values from -6 to 6
- expert_dots: bfloat16 [256, 66], P(('dp', 'expert')), may hold values from -16 to 16
- key_weight: float32 [3072, 512], P(('dp', 'expert')), may hold values from -0.25 to 0.25
- first_moment: float32 [3072, 512], P(('dp', 'expert')), may hold values from -384 to 384
- second_moment: float32 [3072, 512], P(('dp', 'expert')), may hold values from 819.2 to 20480
Outputs:
- input_grad: bfloat16 [4096, 3072], P(('dp', 'expert'))
- new_key_weight: float32 [3072, 512], P(('dp', 'expert'))
- new_first_moment: float32 [3072, 512], P(('dp', 'expert'))
- new_second_moment: float32 [3072, 512], P(('dp', 'expert'))
The draws below stay inside these ranges and needn't reach their ends.
Inputs may be any that keep to these rules, and one draw needn't show every extreme that they name: `routing`: each token names 4 different experts. The 128 tokens of one device name any one expert at most 66 times, and that bound is reached.
All inputs are finite; a program needn't handle non-finite values.
Results may differ from the reference program's by a relative error of at most 0.0043.
Values may be sent and summed in bfloat16 or wider, within the bound.
A program may use at most 64 MiB of HBM per device.

```python
import math
import jax
import jax.numpy as jnp
import numpy as np
from jax import lax

D = 3072
TOP = 4
ADAM_STEP = 10
TOK_DEV = 128
EXPERTS = 8
KCOLS = 512
CAP = 66
TOKENS = 4096
N_DP = 4
N_EXPERT = 8


def strengthened(entries, rng, source, target, parts, factor):
    def block_of(dim):
        return (jnp.arange(entries.shape[dim]) // (entries.shape[dim] // parts)).reshape((-1,) + (1,) * (entries.ndim - 1 - dim))

    first = jax.random.permutation(rng, parts)[block_of(target)]
    far = (block_of(target) + parts // 2) % parts
    return jnp.where((block_of(source) == first) | (block_of(source) == far), factor * entries, entries)


def levels(key, extent, split, smallest, top_value):
    level, own = 1.0, jax.random.fold_in(key, 6)
    for dim, shards_of in split:
        draws = jnp.exp(jax.random.uniform(jax.random.fold_in(own, dim), (shards_of,), jnp.float32, smallest / len(split), top_value / len(split)))
        level = level * jnp.repeat(draws, extent[dim] // shards_of).reshape([-1 if axis == dim else 1 for axis in range(len(extent))])
    return level


def shared_out(stream_key, own, number, rows, number_of, top, bound, lean):
    sequence = jax.random.permutation(stream_key, number_of)
    crowded, ordinary = portions_of(number_of, rows * top, bound, lean, True), portions_of(number_of, rows * top, bound, lean, False)
    places = jnp.arange(number_of)

    def named(tallies, turn):
        used = int((tallies > 0).sum())
        fixed = max(1, used // 4)
        shifted = fixed + (places - fixed + turn * (used - fixed)) % max(1, number_of - fixed)
        return jnp.zeros((number_of,), jnp.int32).at[sequence[jnp.where(places < fixed, places, shifted)]].set(jnp.asarray(tallies, jnp.int32))

    tallies = jnp.where(number % 4 == 0, named(crowded, number // 4), named(ordinary, number - number // 4 - 1))
    mixed = jax.random.permutation(jax.random.fold_in(own, 3), number_of)
    donor, taker = mixed[0:number_of // 2 * 2:2], mixed[1:number_of // 2 * 2:2]
    room = jnp.minimum(tallies[donor] - 1, bound - tallies[taker]) // 2
    room = jnp.where((donor == sequence[0]) | (taker == sequence[0]) | (tallies[taker] == 0), 0, jnp.maximum(room, 0))
    shifted = jax.random.randint(jax.random.fold_in(own, 4), (number_of // 2,), 0, 1 << 20) % (room + 1)
    tallies = tallies.at[donor].add(-shifted).at[taker].add(shifted)
    items = jnp.searchsorted(jnp.cumsum(tallies), jnp.arange(rows * top), side="right").astype(jnp.int32)
    grid = items.reshape(top, rows).T
    grid = grid[jax.random.permutation(jax.random.fold_in(own, 1), rows)]
    turn = jax.random.randint(jax.random.fold_in(own, 2), (rows, 1), 0, top)
    return jnp.take_along_axis(grid, (jnp.arange(top)[None, :] + turn) % top, axis=1)


def portions_of(amount, total, limit, slope, full):
    portions = [(1 << 20) // math.isqrt(standing ** slope) + 1 for standing in range(1, amount + 1)]
    largest = limit if full else min(limit, max(-(-total // amount), total * portions[0] // sum(portions)))
    least = 1 if total - largest >= amount - 1 else 0
    holding, rest = [largest] + [least] * (amount - 1), total - largest - least * (amount - 1)
    while rest > 0:
        free = [i for i in range(1, amount) if holding[i] < largest] or [i for i in range(1, amount) if holding[i] < limit]
        mass, left = sum([portions[i] for i in free]), rest
        for i in free:
            more = min(limit - holding[i], max(1, left * portions[i] // mass), rest)
            holding[i] = holding[i] + more
            rest = rest - more
    return np.array(holding)


def centred(key, dims, spread, limit, cuts=(), kind=jnp.bfloat16):
    values = jax.random.normal(key, dims, jnp.float32) * spread
    if len(cuts) > 0:
        values = levels(key, dims, cuts, -0.22, 0.18) * values
    return jnp.clip(values, min=-limit, max=limit).astype(kind)


def gaussian_with(key, shape, scale, limit, split, heavy, kind=jnp.bfloat16):
    drawn = scale * jax.random.normal(key, shape, jnp.float32)
    if split:
        drawn = drawn * levels(key, shape, split, -0.22, 0.18)
    return jnp.clip(strengthened(drawn, jax.random.fold_in(key, 3), *heavy), -limit, limit).astype(kind)


def setup_inputs(seed: int = 0) -> dict:
    seeds = jax.random.split(jax.random.key(seed), 11)
    attn_input = gaussian_with(seeds[0], (TOKENS, D), 1.0, 6.0, ((0, 32),), (0, 1, 32, 2.75))
    key_cot = centred(seeds[1], (TOKENS, KCOLS), 1.0, 6.0, ((0, 32),))
    routing_keys = jax.random.split(jax.random.fold_in(seeds[2], 1), TOKENS // TOK_DEV)
    routing_turns = jax.random.permutation(jax.random.fold_in(seeds[2], 3), TOKENS // TOK_DEV)
    routing = jax.vmap(lambda own, number: shared_out(jax.random.fold_in(seeds[2], 2), own, number, TOK_DEV, EXPERTS, TOP, CAP, 1))(routing_keys, routing_turns).reshape((TOKENS, TOP))
    router_base = jnp.clip(jax.random.uniform(seeds[3], (TOKENS, EXPERTS), jnp.float32, -1.5, 1.5) * levels(seeds[3], (TOKENS, EXPERTS), ((0, 32),), -0.4, 0.0), -1.5, 1.5)
    router_weight = centred(seeds[4], (D, EXPERTS), EXPERTS ** -0.5, 2.0)
    expert_rows = centred(seeds[5], (N_DP * EXPERTS * EXPERTS, CAP, D), 1.0, 6.0, ((0, 32),))
    expert_dots = centred(seeds[6], (N_DP * EXPERTS * EXPERTS, CAP), 4.0, 16.0, ((0, 32),))
    key_weight = centred(seeds[7], (D, KCOLS), KCOLS ** -0.5, 0.25, ((0, 32),), jnp.float32)
    first_moment = centred(seeds[8], (D, KCOLS), (TOKENS ** 0.5), 384.0, ((0, 32),), jnp.float32)
    second_moment = jnp.clip(jnp.exp(math.log(20480.0) - 3.218876 * jax.random.uniform(seeds[9], (D, KCOLS), jnp.float32) ** levels(seeds[9], (D, KCOLS), ((0, 32),), -0.2, 0.2)), 819.2, 20480.0)
    return {"attn_input": attn_input, "key_cot": key_cot, "routing": routing, "router_base": router_base, "router_weight": router_weight, "expert_rows": expert_rows, "expert_dots": expert_dots, "key_weight": key_weight, "first_moment": first_moment, "second_moment": second_moment}


beta_one = 0.9
beta_two = 0.95
epsilon = 1e-08
learn_rate = 0.005
decay_rate = 0.1
routed_offset = 3.5

def route_slots(routing, experts, capacity):
    choose = (routing[:, :, None] == jnp.arange(experts, dtype=jnp.int32)[None, None, :]).astype(jnp.int32)
    per_expert = lax.optimization_barrier(jnp.sum(choose, axis=1))
    before = jnp.cumsum(per_expert, axis=0) - per_expert
    slots = lax.optimization_barrier(jnp.sum(choose * before[:, None, :], axis=2))
    return (choose, routing * capacity + slots)

def combine(routing, router_base, returned, returned_dots, router_weight):
    experts, capacity, features = returned.shape
    choose, flat_index = route_slots(routing, experts, capacity)
    routed_mask = lax.optimization_barrier(jnp.sum(choose, axis=1)).astype(jnp.float32)
    router_probs = jax.nn.softmax(router_base + routed_offset * routed_mask, axis=-1)
    picked = jnp.take(returned.reshape(experts * capacity, features), flat_index, axis=0)
    inner = jnp.take(returned_dots.reshape(experts * capacity), flat_index, axis=0).astype(jnp.float32)
    chosen = jnp.take_along_axis(router_probs, routing, axis=1)
    chosen_sum = lax.optimization_barrier(jnp.sum(chosen, axis=1, keepdims=True))
    gate_share = chosen / chosen_sum
    mixed = gate_share[:, 0:1] * picked[:, 0].astype(jnp.float32)
    for position in range(1, routing.shape[1]):
        mixed = mixed + gate_share[:, position:position + 1] * picked[:, position].astype(jnp.float32)
    mean_inner = lax.optimization_barrier(jnp.sum(gate_share * inner, axis=1, keepdims=True))
    d_chosen = (inner - mean_inner) / chosen_sum
    d_probs = lax.optimization_barrier(jnp.sum(choose.astype(jnp.float32) * d_chosen[:, :, None], axis=1))
    d_logits = router_probs * (d_probs - lax.optimization_barrier(jnp.sum(router_probs * d_probs, axis=1, keepdims=True)))
    router_term = jnp.dot(d_logits, router_weight.astype(jnp.float32).T, precision=lax.Precision.HIGHEST)
    return mixed + router_term

def adamw(weight, first, second, grad):
    new_first = beta_one * first + (1.0 - beta_one) * grad
    new_second = beta_two * second + (1.0 - beta_two) * grad * grad
    first_hat = new_first / (1.0 - beta_one ** ADAM_STEP)
    second_hat = new_second / (1.0 - beta_two ** ADAM_STEP)
    new_weight = weight - learn_rate * (first_hat / (jnp.sqrt(second_hat) + epsilon) + decay_rate * weight)
    return (new_weight, new_first, new_second)

def reference(attn_input, key_cot, routing, router_base, router_weight, expert_rows, expert_dots, key_weight, first_moment, second_moment):
    devices = N_DP * N_EXPERT
    rows_all = expert_rows.reshape(N_DP, EXPERTS, EXPERTS, CAP, D)
    dots_all = expert_dots.reshape(N_DP, EXPERTS, EXPERTS, CAP)
    inputs = attn_input.reshape(devices, TOK_DEV, D)
    cotangents = key_cot.reshape(devices, TOK_DEV, KCOLS)
    routes = routing.reshape(devices, TOK_DEV, TOP)
    base_all = router_base.reshape(devices, TOK_DEV, EXPERTS)
    key_wide = key_weight.astype(jnp.bfloat16).astype(jnp.float32)

    def one_device(running, index):
        cycle_index = index // N_EXPERT
        source = index % N_EXPERT
        returned = lax.dynamic_index_in_dim(rows_all, cycle_index, 0, False)
        returned = lax.dynamic_index_in_dim(returned, source, 1, False)
        returned_dots = lax.dynamic_index_in_dim(dots_all, cycle_index, 0, False)
        returned_dots = lax.dynamic_index_in_dim(returned_dots, source, 1, False)
        own_routes = lax.dynamic_index_in_dim(routes, index, 0, False)
        own_base = lax.dynamic_index_in_dim(base_all, index, 0, False)
        cotangent = lax.dynamic_index_in_dim(cotangents, index, 0, False).astype(jnp.float32)
        own_input = lax.dynamic_index_in_dim(inputs, index, 0, False).astype(jnp.float32)
        moe_term = combine(own_routes, own_base, returned, returned_dots, router_weight)
        key_term = jnp.dot(cotangent, key_wide.T, precision=lax.Precision.HIGHEST)
        grad_rows = (moe_term + key_term).astype(jnp.bfloat16)
        partial_grad = jnp.dot(own_input.T, cotangent, precision=lax.Precision.HIGHEST)
        partial_grad = lax.optimization_barrier(partial_grad.astype(jnp.bfloat16)).astype(jnp.float32)
        return (running + partial_grad, grad_rows)
    key_grad, grads = lax.scan(one_device, jnp.zeros((D, KCOLS), jnp.float32), jnp.arange(devices, dtype=jnp.int32))
    input_grad = grads.reshape(TOKENS, D)
    new_key_weight, new_first_moment, new_second_moment = adamw(key_weight, first_moment, second_moment, key_grad)
    return (input_grad, new_key_weight, new_first_moment, new_second_moment)
```

```python
import functools

import jax
import jax.numpy as jnp
from jax import lax
from jax.experimental import pallas as pl
from jax.experimental.pallas import tpu as pltpu
from jax.sharding import PartitionSpec as P

ADAM_STEP = 10


beta_one = 0.9
beta_two = 0.95
epsilon = 1e-08
learn_rate = 0.005
decay_rate = 0.1
routed_offset = 3.5


def route_slots(routing, experts, capacity):
    choose = (routing[:, :, None] == jnp.arange(experts, dtype=jnp.int32)[None, None, :]).astype(
        jnp.int32
    )
    per_expert = jnp.sum(choose, axis=1)
    before = jnp.cumsum(per_expert, axis=0) - per_expert
    slots = jnp.sum(choose * before[:, None, :], axis=2)
    return (choose, routing * capacity + slots)


def combine(routing, router_base, returned, returned_dots, router_weight):
    experts, capacity, features = returned.shape
    choose, flat_index = route_slots(routing, experts, capacity)
    routed_mask = jnp.sum(choose, axis=1).astype(jnp.float32)
    router_probs = jax.nn.softmax(router_base + routed_offset * routed_mask, axis=-1)
    picked = jnp.take(returned.reshape(experts * capacity, features), flat_index, axis=0)
    inner = jnp.take(returned_dots.reshape(experts * capacity), flat_index, axis=0).astype(
        jnp.float32
    )
    chosen = jnp.take_along_axis(router_probs, routing, axis=1)
    chosen_sum = jnp.sum(chosen, axis=1, keepdims=True)
    gate_share = chosen / chosen_sum
    mixed = gate_share[:, 0:1] * picked[:, 0].astype(jnp.float32)
    for position in range(1, routing.shape[1]):
        mixed = mixed + gate_share[:, position : position + 1] * picked[:, position].astype(
            jnp.float32
        )
    mean_inner = jnp.sum(gate_share * inner, axis=1, keepdims=True)
    d_chosen = (inner - mean_inner) / chosen_sum
    d_probs = jnp.sum(choose.astype(jnp.float32) * d_chosen[:, :, None], axis=1)
    d_logits = router_probs * (d_probs - jnp.sum(router_probs * d_probs, axis=1, keepdims=True))
    router_term = jnp.dot(
        d_logits, router_weight.astype(jnp.float32).T, precision=lax.Precision.HIGHEST
    )
    return mixed + router_term


def adamw(weight, first, second, grad):
    new_first = beta_one * first + (1.0 - beta_one) * grad
    new_second = beta_two * second + (1.0 - beta_two) * grad * grad
    first_hat = new_first / (1.0 - beta_one**ADAM_STEP)
    second_hat = new_second / (1.0 - beta_two**ADAM_STEP)
    new_weight = weight - learn_rate * (
        first_hat / (jnp.sqrt(second_hat) + epsilon) + decay_rate * weight
    )
    return (new_weight, new_first, new_second)


def local(
    attn_input,
    key_cot,
    routing,
    router_base,
    router_weight,
    expert_rows,
    expert_dots,
    key_weight,
    first_moment,
    second_moment,
):
    returned, returned_dots = (
        lax.all_to_all(expert_rows, "expert", split_axis=0, concat_axis=0, tiled=True),
        lax.all_to_all(expert_dots, "expert", split_axis=0, concat_axis=0, tiled=True),
    )
    moe_term = combine(routing, router_base, returned, returned_dots, router_weight)
    key_term = lax.dot_general(
        key_cot,
        lax.all_gather(key_weight.astype(jnp.bfloat16), ("dp", "expert"), axis=0, tiled=True),
        (((1,), (1,)), ((), ())),
        preferred_element_type=jnp.float32,
    )
    input_grad = (moe_term + key_term).astype(jnp.bfloat16)
    partial_grad = lax.dot_general(
        attn_input, key_cot, (((0,), (0,)), ((), ())), preferred_element_type=jnp.float32
    )
    cycle_size = lax.axis_size("dp")
    group_size = lax.axis_size("expert")
    shard_rows = key_weight.shape[0]
    stacked = partial_grad.reshape(cycle_size, group_size * shard_rows, partial_grad.shape[1])
    halfway = lax.psum_scatter(stacked.astype(jnp.bfloat16), "dp", scatter_dimension=0, tiled=True)
    summed = lax.psum_scatter(halfway, "expert", scatter_dimension=1, tiled=True).astype(
        jnp.float32
    )
    key_grad = summed.reshape(shard_rows, partial_grad.shape[1])
    new_key_weight, new_first_moment, new_second_moment = adamw(
        key_weight, first_moment, second_moment, key_grad
    )
    return (input_grad, new_key_weight, new_first_moment, new_second_moment)


MESH = pl.DeviceIdType.MESH
CONTRACT_FIRST = (((0,), (0,)), ((), ()))
CONTRACT_LAST = (((1,), (1,)), ((), ()))


def split_rows(values):
    high = values.astype(jnp.bfloat16)
    low = (values - high.astype(jnp.float32)).astype(jnp.bfloat16)
    return jnp.concatenate([high, low], axis=0)


def fused(
    attn_hbm,
    cot_ref,
    routing_ref,
    base_ref,
    router_ref,
    rows_hbm,
    dots_ref,
    weight_ref,
    first_ref,
    second_ref,
    out_ref,
    new_weight_ref,
    new_first_ref,
    new_second_ref,
    attn_pair,
    cot_pair,
    rows_got,
    dots_send,
    dots_got,
    wide,
    grad_send,
    grad_got,
    grad_own,
    cross_send,
    cross_got,
    total,
    half_got,
    share,
    acc,
    rows_ss,
    rows_rs,
    dots_ss,
    dots_rs,
    pair_ss,
    pair_rs,
    wz_ss,
    wz_rs,
    wx_ss,
    wx_rs,
    wc_ss,
    wc_rs,
    gz_ss,
    gz_rs,
    gx_ss,
    gx_rs,
    gc_ss,
    gc_rs,
    local_sem,
):
    tokens, features = acc.shape
    experts, capacity, _ = rows_got.shape
    layers, slab, keys = wide.shape
    shard = weight_ref.shape[0]
    half = keys // 2
    z, e = lax.axis_index("dp"), lax.axis_index("expert")
    y, x, c = e // 4, (e // 2) % 2, e % 2

    def peer(r):
        return ((y + r // 4) % 2) * 4 + ((x + (r // 2) % 2) % 2) * 2 + (c + r % 2) % 2

    def rows_of(owner):
        return pl.ds(pl.multiple_of(owner * shard, 32), shard)

    def columns(start, size):
        return pl.ds(pl.multiple_of(start, 256), size)

    def remote(src, dst, send_sem, recv_sem, to):
        copy = pltpu.make_async_remote_copy(
            src_ref=src,
            dst_ref=dst,
            send_sem=send_sem,
            recv_sem=recv_sem,
            device_id=to,
            device_id_type=MESH,
        )
        copy.start()
        return copy

    barrier = pltpu.get_barrier_semaphore()
    for r in range(1, experts):
        pl.semaphore_signal(barrier, inc=1, device_id=(z, peer(r)), device_id_type=MESH)
    for rz in range(1, layers):
        pl.semaphore_signal(
            barrier, inc=1, device_id=((z + rz) % layers, e), device_id_type=MESH
        )
    own_attn = pltpu.make_async_copy(attn_hbm, attn_pair.at[pl.ds(0, tokens)], local_sem.at[0])
    own_attn.start()
    own_rows = pltpu.make_async_copy(rows_hbm.at[e], rows_got.at[0], local_sem.at[1])
    own_rows.start()
    wide[z, rows_of(e), :] = weight_ref[...].astype(jnp.bfloat16)
    dots_all = dots_ref[...].astype(jnp.float32)
    dots_send[...] = jnp.zeros_like(dots_send)
    for j in range(experts):
        dots_send[j, :, 0:capacity] = jnp.broadcast_to(dots_all[j : j + 1, :], (8, capacity))
    cot_pair[0:tokens, :] = cot_ref[:, columns(c * half, half)]
    pl.semaphore_wait(barrier, experts - 1 + layers - 1)

    twin = (z, peer(1))
    pair = [
        remote(
            attn_hbm, attn_pair.at[pl.ds(tokens, tokens)], pair_ss.at[0], pair_rs.at[0], twin
        ),
        remote(
            cot_ref.at[:, columns((1 - c) * half, half)],
            cot_pair.at[pl.ds(tokens, tokens)],
            pair_ss.at[1],
            pair_rs.at[1],
            twin,
        ),
    ]
    mine = wide.at[z, rows_of(e)]
    along = [
        remote(mine, mine, wz_ss.at[rz], wz_rs.at[rz], ((z + rz) % layers, e))
        for rz in range(1, layers)
    ]
    dots = {}
    for r in range(1, experts):
        dots[r] = remote(
            dots_send.at[peer(r)], dots_got.at[r], dots_ss.at[r], dots_rs.at[r], (z, peer(r))
        )
    rows = {}
    for r in range(1, experts):
        rows[r] = remote(
            rows_hbm.at[peer(r)], rows_got.at[r], rows_ss.at[r], rows_rs.at[r], (z, peer(r))
        )

    own_attn.wait()
    for copy in pair:
        copy.wait_recv()

    def partial(layer):
        return lax.dot_general(
            attn_pair[:, columns(layer * slab, slab)],
            cot_pair[...],
            CONTRACT_FIRST,
            preferred_element_type=jnp.float32,
        )

    outward = {}
    for rz in (2, 1, 3):
        to = (z + rz) % layers
        grad_send[rz] = partial(to).astype(jnp.bfloat16)
        outward[rz] = remote(
            grad_send.at[rz], grad_got.at[rz], gz_ss.at[rz], gz_rs.at[rz], (to, e)
        )
    grad_own[...] = partial(z)

    lanes = lax.broadcasted_iota(jnp.int32, (tokens, experts), 1)
    routing = routing_ref[...]
    choose = jnp.zeros((tokens, experts), jnp.float32)
    for k in range(routing.shape[1]):
        choose = choose + (routing[:, k : k + 1] == lanes).astype(jnp.float32)
    earlier = (
        lax.broadcasted_iota(jnp.int32, (tokens, tokens), 1)
        < lax.broadcasted_iota(jnp.int32, (tokens, tokens), 0)
    ).astype(jnp.bfloat16)
    before = jnp.dot(
        earlier, choose.astype(jnp.bfloat16), preferred_element_type=jnp.float32
    ).astype(jnp.int32)
    place = jnp.where(choose > 0.0, before, -1)
    logits = base_ref[...] + routed_offset * choose
    raised = jnp.exp(logits - jnp.max(logits, axis=1, keepdims=True))
    probs = raised / jnp.sum(raised, axis=1, keepdims=True)
    chosen = probs * choose
    chosen_sum = jnp.sum(chosen, axis=1, keepdims=True)
    gate = chosen / chosen_sum

    for copy in along:
        copy.wait_recv()
    column = wide.at[:, rows_of(e)]
    across = {
        q: remote(column, column, wx_ss.at[q], wx_rs.at[q], (z, peer(2 * q)))
        for q in range(1, 4)
    }
    swap = {0: remote(column, column, wc_ss.at[0], wc_rs.at[0], twin)}

    inner = jnp.zeros((tokens, experts), jnp.float32)
    slots = lax.broadcasted_iota(jnp.int32, (tokens, capacity), 1)
    for r in range(experts):
        if r > 0:
            dots[r].wait_recv()
            got = dots_got[r, 0:1, 0:capacity]
        else:
            got = dots_send[e, 0:1, 0:capacity]
        this = lanes == peer(r)
        place_r = jnp.sum(jnp.where(this, place, 0), axis=1, keepdims=True)
        gate_r = jnp.sum(jnp.where(this, gate, 0.0), axis=1, keepdims=True)
        hit = slots == place_r
        share[r] = split_rows(jnp.where(hit, gate_r, 0.0))
        inner_r = jnp.sum(jnp.where(hit, got, 0.0), axis=1, keepdims=True)
        inner = inner + jnp.where(this, inner_r, 0.0)
    mean_inner = jnp.sum(gate * inner, axis=1, keepdims=True)
    d_probs = choose * (inner - mean_inner) / chosen_sum
    d_logits = probs * (d_probs - jnp.sum(probs * d_probs, axis=1, keepdims=True))
    d_parts = split_rows(d_logits)

    def router_tile(i, _):
        here = columns(i * slab, slab)
        both = lax.dot_general(
            d_parts, router_ref[here, :], CONTRACT_LAST, preferred_element_type=jnp.float32
        )
        acc[:, here] = both[:tokens] + both[tokens:]
        return 0

    lax.fori_loop(0, layers, router_tile, 0)

    def add_rows(r):
        def tile(i, _):
            here = columns(i * slab, slab)
            both = jnp.dot(
                share[r], rows_got[r, :, here], preferred_element_type=jnp.float32
            )
            acc[:, here] += both[:tokens] + both[tokens:]
            return 0

        lax.fori_loop(0, layers, tile, 0)

    own_rows.wait()
    add_rows(0)
    rows[1].wait_recv()
    add_rows(1)

    for q in range(1, 4):
        across[q].wait_recv()
        block = wide.at[:, rows_of(peer(2 * q))]
        swap[q] = remote(block, block, wc_ss.at[q], wc_rs.at[q], twin)

    for rz in range(1, layers):
        outward[rz].wait_recv()
    grad_own[...] = (
        grad_own[...]
        + grad_got[1].astype(jnp.float32)
        + grad_got[2].astype(jnp.float32)
        + grad_got[3].astype(jnp.float32)
    )
    inward = {}
    for q in range(1, 4):
        chip = pl.ds(pl.multiple_of((peer(2 * q) // 2) * (2 * shard), 32), 2 * shard)
        cross_send[q] = grad_own[chip, :].astype(jnp.bfloat16)
        inward[q] = remote(
            cross_send.at[q], cross_got.at[q], gx_ss.at[q], gx_rs.at[q], (z, peer(2 * q))
        )

    for q in range(4):
        swap[q].wait_recv()

    def key_tile(i, _):
        here = columns(i * slab, slab)
        acc[:, here] += lax.dot_general(
            cot_ref[...], wide[i], CONTRACT_LAST, preferred_element_type=jnp.float32
        )
        return 0

    lax.fori_loop(0, layers, key_tile, 0)

    for r in (2, 3, 4, 5):
        rows[r].wait_recv()
        add_rows(r)

    for q in range(1, 4):
        inward[q].wait_recv()
    chip = pl.ds(pl.multiple_of((e // 2) * (2 * shard), 32), 2 * shard)
    total[...] = (
        grad_own[chip, :]
        + cross_got[1].astype(jnp.float32)
        + cross_got[2].astype(jnp.float32)
        + cross_got[3].astype(jnp.float32)
    )
    last = remote(total.at[rows_of(1 - c)], half_got, gc_ss, gc_rs, twin)

    def update(here, grad):
        weight, first, second = adamw(
            weight_ref[:, here], first_ref[:, here], second_ref[:, here], grad
        )
        new_weight_ref[:, here] = weight
        new_first_ref[:, here] = first
        new_second_ref[:, here] = second

    update(columns(c * half, half), total[rows_of(c), :])

    for r in (6, 7):
        rows[r].wait_recv()
        add_rows(r)
    out_ref[...] = acc[...].astype(jnp.bfloat16)
    last.wait_recv()
    update(columns((1 - c) * half, half), half_got[...])

    for copy in [*pair, *along, *dots.values(), *rows.values(), *outward.values()]:
        copy.wait_send()
    for copy in [*across.values(), *swap.values(), *inward.values(), last]:
        copy.wait_send()


def fused_local(
    attn_input,
    key_cot,
    routing,
    router_base,
    router_weight,
    expert_rows,
    expert_dots,
    key_weight,
    first_moment,
    second_moment,
):
    tokens, features = attn_input.shape
    experts, capacity, _ = expert_rows.shape
    shard, keys = key_weight.shape
    layers = lax.axis_size("dp")
    slab, half = features // layers, keys // 2
    b16, f32 = jnp.bfloat16, jnp.float32
    vmem, anywhere = pl.BlockSpec(memory_space=pltpu.VMEM), pl.BlockSpec(memory_space=pl.ANY)
    dma = pltpu.SemaphoreType.DMA
    return pl.pallas_call(
        fused,
        out_shape=(
            jax.ShapeDtypeStruct((tokens, features), b16),
            jax.ShapeDtypeStruct((shard, keys), f32),
            jax.ShapeDtypeStruct((shard, keys), f32),
            jax.ShapeDtypeStruct((shard, keys), f32),
        ),
        in_specs=[anywhere, vmem, vmem, vmem, vmem, anywhere, vmem, vmem, vmem, vmem],
        out_specs=[vmem] * 4,
        scratch_shapes=[
            pltpu.VMEM((2 * tokens, features), b16),
            pltpu.VMEM((2 * tokens, half), b16),
            pltpu.VMEM((experts, capacity, features), b16),
            pltpu.VMEM((experts, 8, 128), f32),
            pltpu.VMEM((experts, 8, 128), f32),
            pltpu.VMEM((layers, slab, keys), b16),
            pltpu.VMEM((layers, slab, half), b16),
            pltpu.VMEM((layers, slab, half), b16),
            pltpu.VMEM((slab, half), f32),
            pltpu.VMEM((4, 2 * shard, half), b16),
            pltpu.VMEM((4, 2 * shard, half), b16),
            pltpu.VMEM((2 * shard, half), f32),
            pltpu.VMEM((shard, half), f32),
            pltpu.VMEM((experts, 2 * tokens, capacity), b16),
            pltpu.VMEM((tokens, features), f32),
            dma((experts,)),
            dma((experts,)),
            dma((experts,)),
            dma((experts,)),
            dma((2,)),
            dma((2,)),
            dma((layers,)),
            dma((layers,)),
            dma((4,)),
            dma((4,)),
            dma((4,)),
            dma((4,)),
            dma((layers,)),
            dma((layers,)),
            dma((4,)),
            dma((4,)),
            dma,
            dma,
            dma((2,)),
        ],
        compiler_params=pltpu.CompilerParams(
            collective_id=0, has_side_effects=True, vmem_limit_bytes=40 * 1024 * 1024
        ),
        cost_estimate=pl.CostEstimate(
            flops=4 * 10**9, bytes_accessed=10**7, transcendentals=10**5
        ),
    )(
        attn_input,
        key_cot,
        routing,
        router_base,
        router_weight,
        expert_rows,
        expert_dots,
        key_weight,
        first_moment,
        second_moment,
    )


def solution(mesh):
    fits = mesh.shape["dp"] == 4 and mesh.shape["expert"] == 8
    in_specs = (
        P(("dp", "expert"), None),
        P(("dp", "expert"), None),
        P(("dp", "expert"), None),
        P(("dp", "expert"), None),
        P(),
        P(("dp", "expert"), None, None),
        P(("dp", "expert"), None),
        P(("dp", "expert"), None),
        P(("dp", "expert"), None),
        P(("dp", "expert"), None),
    )
    out_specs = (
        P(("dp", "expert"), None),
        P(("dp", "expert"), None),
        P(("dp", "expert"), None),
        P(("dp", "expert"), None),
    )
    return jax.shard_map(
        fused_local if fits else local, mesh=mesh, in_specs=in_specs, out_specs=out_specs, check_vma=False)
```

```python
import jax
import jax.numpy as jnp
from jax import lax
from jax.experimental import pallas as pl
from jax.experimental.pallas import tpu as pltpu
from jax.sharding import PartitionSpec as P

ADAM_STEP = 10


beta_one = 0.9
beta_two = 0.95
epsilon = 1e-08
learn_rate = 0.005
decay_rate = 0.1
routed_offset = 3.5


def route_slots(routing, experts, capacity):
    choose = (routing[:, :, None] == jnp.arange(experts, dtype=jnp.int32)[None, None, :]).astype(
        jnp.int32
    )
    per_expert = jnp.sum(choose, axis=1)
    before = jnp.cumsum(per_expert, axis=0) - per_expert
    slots = jnp.sum(choose * before[:, None, :], axis=2)
    return (choose, routing * capacity + slots)


def combine(routing, router_base, returned, returned_dots, router_weight):
    experts, capacity, features = returned.shape
    choose, flat_index = route_slots(routing, experts, capacity)
    routed_mask = jnp.sum(choose, axis=1).astype(jnp.float32)
    router_probs = jax.nn.softmax(router_base + routed_offset * routed_mask, axis=-1)
    picked = jnp.take(returned.reshape(experts * capacity, features), flat_index, axis=0)
    inner = jnp.take(returned_dots.reshape(experts * capacity), flat_index, axis=0).astype(
        jnp.float32
    )
    chosen = jnp.take_along_axis(router_probs, routing, axis=1)
    chosen_sum = jnp.sum(chosen, axis=1, keepdims=True)
    gate_share = chosen / chosen_sum
    mixed = gate_share[:, 0:1] * picked[:, 0].astype(jnp.float32)
    for position in range(1, routing.shape[1]):
        mixed = mixed + gate_share[:, position : position + 1] * picked[:, position].astype(
            jnp.float32
        )
    mean_inner = jnp.sum(gate_share * inner, axis=1, keepdims=True)
    d_chosen = (inner - mean_inner) / chosen_sum
    d_probs = jnp.sum(choose.astype(jnp.float32) * d_chosen[:, :, None], axis=1)
    d_logits = router_probs * (d_probs - jnp.sum(router_probs * d_probs, axis=1, keepdims=True))
    router_term = jnp.dot(
        d_logits, router_weight.astype(jnp.float32).T, precision=lax.Precision.HIGHEST
    )
    return mixed + router_term


def adamw(weight, first, second, grad):
    new_first = beta_one * first + (1.0 - beta_one) * grad
    new_second = beta_two * second + (1.0 - beta_two) * grad * grad
    first_hat = new_first / (1.0 - beta_one**ADAM_STEP)
    second_hat = new_second / (1.0 - beta_two**ADAM_STEP)
    new_weight = weight - learn_rate * (
        first_hat / (jnp.sqrt(second_hat) + epsilon) + decay_rate * weight
    )
    return (new_weight, new_first, new_second)


def local(
    attn_input,
    key_cot,
    routing,
    router_base,
    router_weight,
    expert_rows,
    expert_dots,
    key_weight,
    first_moment,
    second_moment,
):
    returned, returned_dots = (
        lax.all_to_all(expert_rows, "expert", split_axis=0, concat_axis=0, tiled=True),
        lax.all_to_all(expert_dots, "expert", split_axis=0, concat_axis=0, tiled=True),
    )
    moe_term = combine(routing, router_base, returned, returned_dots, router_weight)
    key_term = lax.dot_general(
        key_cot,
        lax.all_gather(key_weight.astype(jnp.bfloat16), ("dp", "expert"), axis=0, tiled=True),
        (((1,), (1,)), ((), ())),
        preferred_element_type=jnp.float32,
    )
    input_grad = (moe_term + key_term).astype(jnp.bfloat16)
    partial_grad = lax.dot_general(
        attn_input, key_cot, (((0,), (0,)), ((), ())), preferred_element_type=jnp.float32
    )
    cycle_size = lax.axis_size("dp")
    group_size = lax.axis_size("expert")
    shard_rows = key_weight.shape[0]
    stacked = partial_grad.reshape(cycle_size, group_size * shard_rows, partial_grad.shape[1])
    halfway = lax.psum_scatter(stacked.astype(jnp.bfloat16), "dp", scatter_dimension=0, tiled=True)
    summed = lax.psum_scatter(halfway, "expert", scatter_dimension=1, tiled=True).astype(
        jnp.float32
    )
    key_grad = summed.reshape(shard_rows, partial_grad.shape[1])
    new_key_weight, new_first_moment, new_second_moment = adamw(
        key_weight, first_moment, second_moment, key_grad
    )
    return (input_grad, new_key_weight, new_first_moment, new_second_moment)


MESH = pl.DeviceIdType.MESH
CONTRACT_FIRST = (((0,), (0,)), ((), ()))
CONTRACT_LAST = (((1,), (1,)), ((), ()))
SLOTS = 80


def split_columns(values):
    high = values.astype(jnp.bfloat16)
    low = (values - high.astype(jnp.float32)).astype(jnp.bfloat16)
    return jnp.concatenate([high, low], axis=1)


def fused(
    attn_ref,
    cot_ref,
    routing_ref,
    base_ref,
    router_ref,
    rows_hbm,
    dots_ref,
    weight_ref,
    out_ref,
    grad_ref,
    rows_own,
    picked,
    blocks,
    info_send,
    info_got,
    dots_send,
    dots_got,
    cots,
    attn_send,
    attn_got,
    window,
    part,
    send,
    relay_got,
    x_got,
    y_got,
    grad_send,
    grad_got,
    local_sem,
    info_ss,
    info_rs,
    rows_ss,
    rows_rs,
    dots_ss,
    dots_rs,
    cot_ss,
    cot_rs,
    twin_ss,
    twin_rs,
    attn_ss,
    attn_rs,
    wz_ss,
    wz_rs,
    wt_ss,
    wt_rs,
    part_ss,
    part_rs,
    gz_ss,
    gz_rs,
):
    tokens, features = out_ref.shape
    experts, capacity = dots_ref.shape
    shard, keys = weight_ref.shape
    layers = window.shape[0]
    slab = features // layers
    half = features // 2
    z, e = lax.axis_index("dp"), lax.axis_index("expert")
    y, x, c = e // 4, (e // 2) % 2, e % 2
    chip = e // 2

    def peer(r):
        return ((y + r // 4) % 2) * 4 + ((x + (r // 2) % 2) % 2) * 2 + (c + r % 2) % 2

    def columns(start, size):
        return pl.ds(pl.multiple_of(start, 128), size)

    def remote(src, dst, send_sem, recv_sem, to):
        copy = pltpu.make_async_remote_copy(
            src_ref=src,
            dst_ref=dst,
            send_sem=send_sem,
            recv_sem=recv_sem,
            device_id=to,
            device_id_type=MESH,
        )
        copy.start()
        return copy

    barrier = pltpu.get_barrier_semaphore()
    for r in range(1, experts):
        pl.semaphore_signal(barrier, inc=1, device_id=(z, peer(r)), device_id_type=MESH)
    for rz in range(1, layers):
        pl.semaphore_signal(
            barrier, inc=1, device_id=((z + rz) % layers, e), device_id_type=MESH
        )
    load = pltpu.make_async_copy(rows_hbm, rows_own, local_sem)
    load.start()

    shift = 64 * (chip % 2)

    def window_rows(core):
        return pl.ds(pl.multiple_of(shift + core * shard, 32), shard)

    window[z, window_rows(c), :] = weight_ref[...].astype(jnp.bfloat16)
    spare = pl.ds(pl.multiple_of(2 * shard * (1 - chip % 2), 64), 64)
    for i in range(layers):
        window[i, spare, :] = jnp.zeros((64, keys), jnp.bfloat16)

    routing = routing_ref[...]
    names = lax.broadcasted_iota(jnp.int32, (experts, tokens), 0)
    choose = jnp.zeros((experts, tokens), jnp.float32)
    for k in range(routing.shape[0]):
        choose = choose + (routing[k : k + 1, :] == names).astype(jnp.float32)
    earlier = (
        lax.broadcasted_iota(jnp.int32, (tokens, tokens), 0)
        < lax.broadcasted_iota(jnp.int32, (tokens, tokens), 1)
    ).astype(jnp.bfloat16)
    before = jnp.dot(choose.astype(jnp.bfloat16), earlier, preferred_element_type=jnp.float32)
    place = jnp.where(choose > 0.0, before, -1.0)
    logits = base_ref[...] + routed_offset * choose
    raised = jnp.exp(logits - jnp.max(logits, axis=0, keepdims=True))
    probs = raised / jnp.sum(raised, axis=0, keepdims=True)
    chosen = probs * choose
    chosen_sum = jnp.sum(chosen, axis=0, keepdims=True)
    gate = chosen / chosen_sum
    info_send[0] = place
    info_send[1] = gate

    dots_all = dots_ref[...].astype(jnp.float32)
    dots_send[...] = jnp.zeros_like(dots_send)
    for j in range(experts):
        dots_send[j, :, 0:capacity] = jnp.broadcast_to(dots_all[j : j + 1, :], (8, capacity))
    cots[0] = cot_ref[...]
    for j in range(experts):
        attn_send[j] = jnp.concatenate(
            [
                attn_ref[:, i * slab + j * shard : i * slab + (j + 1) * shard]
                for i in range(layers)
            ],
            axis=1,
        )
    attn_got[0] = attn_send[e]
    pl.semaphore_wait(barrier, experts - 1 + layers - 1)

    twin = (z, peer(1))
    info, cot, attn, dots, rows = {}, {}, {}, {}, {}
    for q in (3, 1, 2):
        info[q] = remote(
            info_send, info_got.at[q], info_ss.at[q], info_rs.at[q], (z, peer(2 * q))
        )
    mine = window.at[z, window_rows(c)]
    along = [
        remote(mine, mine, wz_ss.at[rz], wz_rs.at[rz], ((z + rz) % layers, e))
        for rz in range(1, layers)
    ]
    for q in (3, 1, 2):
        cot[q] = remote(
            cot_ref, cots.at[2 * q], cot_ss.at[q], cot_rs.at[q], (z, peer(2 * q))
        )
    for r in (6, 7, 2, 3, 4, 5, 1):
        attn[r] = remote(
            attn_send.at[peer(r)], attn_got.at[r], attn_ss.at[r], attn_rs.at[r], (z, peer(r))
        )
        dots[r] = remote(
            dots_send.at[peer(r)], dots_got.at[r], dots_ss.at[r], dots_rs.at[r], (z, peer(r))
        )

    load.wait()
    cell = lax.broadcasted_iota(jnp.int32, (SLOTS, experts * capacity), 1)
    first_cell = experts * lax.broadcasted_iota(jnp.int32, (SLOTS, experts * capacity), 0)
    pick = jnp.concatenate(
        [
            (cell == first_cell + peer(r)).astype(jnp.float32).astype(jnp.bfloat16)
            for r in (1, 3, 5, 7, 0, 2, 4, 6)
        ],
        axis=0,
    )

    def pick_tile(i, _):
        here = columns(i * slab, slab)
        got = jnp.dot(pick, rows_own[:, here], preferred_element_type=jnp.float32)
        for q in range(4):
            picked[q, :, here] = got[q * SLOTS : (q + 1) * SLOTS].astype(jnp.bfloat16)
            blocks[q, 0:SLOTS, here] = got[(4 + q) * SLOTS : (5 + q) * SLOTS].astype(
                jnp.bfloat16
            )
        return 0

    lax.fori_loop(0, layers, pick_tile, 0)
    for q in (3, 1, 2, 0):
        rows[q] = remote(
            picked.at[q],
            blocks.at[q, pl.ds(SLOTS, SLOTS)],
            rows_ss.at[q],
            rows_rs.at[q],
            twin,
        )

    for copy in along:
        copy.wait_recv()
    column = window.at[:, window_rows(c)]
    swap = remote(column, column, wt_ss, wt_rs, twin)
    forward = {0: remote(cots.at[0], cots.at[1], twin_ss.at[0], twin_rs.at[0], twin)}

    slots = lax.broadcasted_iota(jnp.int32, (SLOTS, tokens), 0)

    def row_of(values, expert):
        return jnp.sum(jnp.where(names == expert, values, 0.0), axis=0, keepdims=True)

    def add_rows(q):
        if q:
            info[q].wait_recv()
            place_q, gate_q = info_got[q, 0], info_got[q, 1]
        else:
            place_q, gate_q = place, gate
        share = jnp.concatenate(
            [
                jnp.where(
                    slots == row_of(place_q, expert).astype(jnp.int32),
                    row_of(gate_q, expert),
                    0.0,
                )
                for expert in (e, peer(1))
            ],
            axis=0,
        )
        share = split_columns(share)
        rows[q].wait_recv()

        def tile(i, _):
            here = columns(i * slab, slab)
            both = lax.dot_general(
                share, blocks[q, :, here], CONTRACT_FIRST, preferred_element_type=jnp.float32
            )
            part[q, :, here] = both[:tokens] + both[tokens:]
            return 0

        lax.fori_loop(0, layers, tile, 0)

    start = (chip * 2 * shard) // 128 * 128
    width = window.shape[1]

    def add_key(q):
        def tile(i, _):
            here = columns(i * slab + start, width)
            part[q, :, here] += lax.dot_general(
                cots[2 * q], window[i], CONTRACT_LAST, preferred_element_type=jnp.float32
            )
            return 0

        lax.fori_loop(0, layers, tile, 0)

    left, right = slice(0, half), slice(half, features)
    to_x, to_y = (z, peer(2)), (z, peer(4))
    parts = []

    def send_part(q, cut, dst, number, to):
        parts.append(
            remote(
                send.at[q, :, pl.ds(cut.start, half)],
                dst.at[:, pl.ds(cut.start, half)],
                part_ss.at[number],
                part_rs.at[number],
                to,
            )
        )

    add_rows(3)
    swap.wait_recv()
    cot[3].wait_recv()
    forward[3] = remote(cots.at[6], cots.at[7], twin_ss.at[3], twin_rs.at[3], twin)
    add_key(3)
    send[3] = part[3].astype(jnp.bfloat16)
    send_part(3, left, relay_got, 0, to_x)
    send_part(3, right, relay_got, 1, to_y)
    for q, cut, dst, to in ((1, left, x_got, to_x), (2, right, y_got, to_y)):
        add_rows(q)
        cot[q].wait_recv()
        forward[q] = remote(
            cots.at[2 * q], cots.at[2 * q + 1], twin_ss.at[q], twin_rs.at[q], twin
        )
        add_key(q)
        send[q, :, cut] = part[q, :, cut].astype(jnp.bfloat16)
        send_part(q, cut, dst, q + 1, to)

    for q in range(4):
        forward[q].wait_recv()
    for r in range(1, experts):
        attn[r].wait_recv()
    grad = lax.dot_general(
        attn_got[...].reshape(experts * tokens, layers * shard),
        cots[...].reshape(experts * tokens, keys),
        CONTRACT_FIRST,
        preferred_element_type=jnp.float32,
    )
    grad_send[...] = grad.reshape(layers, shard, keys).astype(jnp.bfloat16)
    outward = {}
    for rz in (2, 1, 3):
        to = (z + rz) % layers
        outward[rz] = remote(
            grad_send.at[to], grad_got.at[rz], gz_ss.at[rz], gz_rs.at[rz], (to, e)
        )
    layer = lax.broadcasted_iota(jnp.int32, (layers, 1, 1), 0)
    grad_ref[...] = jnp.sum(
        jnp.where(layer == z, grad.reshape(layers, shard, keys), 0.0), axis=0
    )

    inner = jnp.zeros((experts, tokens), jnp.float32)
    for r in range(experts):
        if r > 0:
            dots[r].wait_recv()
            got = dots_got[r, :, 0:SLOTS]
        else:
            got = dots_send[e, :, 0:SLOTS]
        expert = peer(r)
        hit = (slots == row_of(place, expert).astype(jnp.int32)).astype(jnp.float32)
        found = jnp.dot(
            got.astype(jnp.bfloat16),
            hit.astype(jnp.bfloat16),
            preferred_element_type=jnp.float32,
        )
        inner = inner + jnp.where(names == expert, found[0:1, :], 0.0)
    mean_inner = jnp.sum(gate * inner, axis=0, keepdims=True)
    d_probs = choose * (inner - mean_inner) / chosen_sum
    d_logits = probs * (d_probs - jnp.sum(probs * d_probs, axis=0, keepdims=True))
    d_parts = split_columns(d_logits)

    add_rows(0)
    add_key(0)

    def router_tile(i, _):
        here = columns(i * slab, slab)
        both = lax.dot_general(
            d_parts, router_ref[:, here], CONTRACT_FIRST, preferred_element_type=jnp.float32
        )
        part[0, :, here] += both[:tokens] + both[tokens:]
        return 0

    lax.fori_loop(0, layers, router_tile, 0)

    parts[0].wait_recv()
    send[2, :, left] = (
        part[2, :, left] + relay_got[:, left].astype(jnp.float32)
    ).astype(jnp.bfloat16)
    send_part(2, left, y_got, 4, to_y)
    parts[1].wait_recv()
    send[1, :, right] = (
        part[1, :, right] + relay_got[:, right].astype(jnp.float32)
    ).astype(jnp.bfloat16)
    send_part(1, right, x_got, 5, to_x)

    for rz in range(1, layers):
        outward[rz].wait_recv()
    grad_ref[...] = (
        grad_ref[...]
        + grad_got[1].astype(jnp.float32)
        + grad_got[2].astype(jnp.float32)
        + grad_got[3].astype(jnp.float32)
    )
    for copy in parts[2:]:
        copy.wait_recv()
    out_ref[...] = (
        part[0] + x_got[...].astype(jnp.float32) + y_got[...].astype(jnp.float32)
    ).astype(jnp.bfloat16)

    for group in (info, cot, attn, dots, rows, forward, outward):
        for copy in group.values():
            copy.wait_send()
    for copy in [*along, swap, *parts]:
        copy.wait_send()


def fused_local(
    attn_input,
    key_cot,
    routing,
    router_base,
    router_weight,
    expert_rows,
    expert_dots,
    key_weight,
    first_moment,
    second_moment,
):
    tokens, features = attn_input.shape
    experts, capacity, _ = expert_rows.shape
    shard, keys = key_weight.shape
    layers = lax.axis_size("dp")
    b16, f32 = jnp.bfloat16, jnp.float32
    vmem, anywhere = pl.BlockSpec(memory_space=pltpu.VMEM), pl.BlockSpec(memory_space=pl.ANY)
    dma = pltpu.SemaphoreType.DMA
    input_grad, key_grad = pl.pallas_call(
        fused,
        out_shape=(
            jax.ShapeDtypeStruct((tokens, features), b16),
            jax.ShapeDtypeStruct((shard, keys), f32),
        ),
        in_specs=[vmem, vmem, vmem, vmem, vmem, anywhere, vmem, vmem],
        out_specs=[vmem] * 2,
        scratch_shapes=[
            pltpu.VMEM((experts * capacity, features), b16),
            pltpu.VMEM((4, SLOTS, features), b16),
            pltpu.VMEM((4, 2 * SLOTS, features), b16),
            pltpu.VMEM((2, experts, tokens), f32),
            pltpu.VMEM((4, 2, experts, tokens), f32),
            pltpu.VMEM((experts, 8, 128), f32),
            pltpu.VMEM((experts, 8, 128), f32),
            pltpu.VMEM((experts, tokens, keys), b16),
            pltpu.VMEM((experts, tokens, layers * shard), b16),
            pltpu.VMEM((experts, tokens, layers * shard), b16),
            pltpu.VMEM((layers, 2 * shard + 64, keys), b16),
            pltpu.VMEM((4, tokens, features), f32),
            pltpu.VMEM((4, tokens, features), b16),
            pltpu.VMEM((tokens, features), b16),
            pltpu.VMEM((tokens, features), b16),
            pltpu.VMEM((tokens, features), b16),
            pltpu.VMEM((layers, shard, keys), b16),
            pltpu.VMEM((layers, shard, keys), b16),
            dma,
            dma((4,)),
            dma((4,)),
            dma((4,)),
            dma((4,)),
            dma((experts,)),
            dma((experts,)),
            dma((4,)),
            dma((4,)),
            dma((4,)),
            dma((4,)),
            dma((experts,)),
            dma((experts,)),
            dma((layers,)),
            dma((layers,)),
            dma,
            dma,
            dma((6,)),
            dma((6,)),
            dma((layers,)),
            dma((layers,)),
        ],
        compiler_params=pltpu.CompilerParams(
            collective_id=0, has_side_effects=True, vmem_limit_bytes=48 * 1024 * 1024
        ),
        cost_estimate=pl.CostEstimate(
            flops=6 * 10**9, bytes_accessed=10**7, transcendentals=10**4
        ),
    )(
        attn_input,
        key_cot,
        routing.T,
        router_base.T,
        router_weight.T,
        expert_rows.transpose(1, 0, 2).reshape(capacity * experts, features),
        expert_dots,
        key_weight,
    )
    return (input_grad, *adamw(key_weight, first_moment, second_moment, key_grad))


def solution(mesh):
    fits = mesh.shape["dp"] == 4 and mesh.shape["expert"] == 8
    in_specs = (
        P(("dp", "expert"), None),
        P(("dp", "expert"), None),
        P(("dp", "expert"), None),
        P(("dp", "expert"), None),
        P(),
        P(("dp", "expert"), None, None),
        P(("dp", "expert"), None),
        P(("dp", "expert"), None),
        P(("dp", "expert"), None),
        P(("dp", "expert"), None),
    )
    out_specs = (
        P(("dp", "expert"), None),
        P(("dp", "expert"), None),
        P(("dp", "expert"), None),
        P(("dp", "expert"), None),
    )
    return jax.shard_map(
        fused_local if fits else local, mesh=mesh, in_specs=in_specs, out_specs=out_specs, check_vma=False)
```

```python
import jax
import jax.numpy as jnp
from jax import lax
from jax.experimental import pallas as pl
from jax.experimental.pallas import tpu as pltpu
from jax.sharding import PartitionSpec as P

ADAM_STEP = 10


beta_one = 0.9
beta_two = 0.95
epsilon = 1e-08
learn_rate = 0.005
decay_rate = 0.1
routed_offset = 3.5


def route_slots(routing, experts, capacity):
    choose = (routing[:, :, None] == jnp.arange(experts, dtype=jnp.int32)[None, None, :]).astype(
        jnp.int32
    )
    per_expert = jnp.sum(choose, axis=1)
    before = jnp.cumsum(per_expert, axis=0) - per_expert
    slots = jnp.sum(choose * before[:, None, :], axis=2)
    return (choose, routing * capacity + slots)


def combine(routing, router_base, returned, returned_dots, router_weight):
    experts, capacity, features = returned.shape
    choose, flat_index = route_slots(routing, experts, capacity)
    routed_mask = jnp.sum(choose, axis=1).astype(jnp.float32)
    router_probs = jax.nn.softmax(router_base + routed_offset * routed_mask, axis=-1)
    picked = jnp.take(returned.reshape(experts * capacity, features), flat_index, axis=0)
    inner = jnp.take(returned_dots.reshape(experts * capacity), flat_index, axis=0).astype(
        jnp.float32
    )
    chosen = jnp.take_along_axis(router_probs, routing, axis=1)
    chosen_sum = jnp.sum(chosen, axis=1, keepdims=True)
    gate_share = chosen / chosen_sum
    mixed = gate_share[:, 0:1] * picked[:, 0].astype(jnp.float32)
    for position in range(1, routing.shape[1]):
        mixed = mixed + gate_share[:, position : position + 1] * picked[:, position].astype(
            jnp.float32
        )
    mean_inner = jnp.sum(gate_share * inner, axis=1, keepdims=True)
    d_chosen = (inner - mean_inner) / chosen_sum
    d_probs = jnp.sum(choose.astype(jnp.float32) * d_chosen[:, :, None], axis=1)
    d_logits = router_probs * (d_probs - jnp.sum(router_probs * d_probs, axis=1, keepdims=True))
    router_term = jnp.dot(
        d_logits, router_weight.astype(jnp.float32).T, precision=lax.Precision.HIGHEST
    )
    return mixed + router_term


def adamw(weight, first, second, grad):
    new_first = beta_one * first + (1.0 - beta_one) * grad
    new_second = beta_two * second + (1.0 - beta_two) * grad * grad
    first_hat = new_first / (1.0 - beta_one**ADAM_STEP)
    second_hat = new_second / (1.0 - beta_two**ADAM_STEP)
    new_weight = weight - learn_rate * (
        first_hat / (jnp.sqrt(second_hat) + epsilon) + decay_rate * weight
    )
    return (new_weight, new_first, new_second)


def local(
    attn_input,
    key_cot,
    routing,
    router_base,
    router_weight,
    expert_rows,
    expert_dots,
    key_weight,
    first_moment,
    second_moment,
):
    returned, returned_dots = (
        lax.all_to_all(expert_rows, "expert", split_axis=0, concat_axis=0, tiled=True),
        lax.all_to_all(expert_dots, "expert", split_axis=0, concat_axis=0, tiled=True),
    )
    moe_term = combine(routing, router_base, returned, returned_dots, router_weight)
    key_term = lax.dot_general(
        key_cot,
        lax.all_gather(key_weight.astype(jnp.bfloat16), ("dp", "expert"), axis=0, tiled=True),
        (((1,), (1,)), ((), ())),
        preferred_element_type=jnp.float32,
    )
    input_grad = (moe_term + key_term).astype(jnp.bfloat16)
    partial_grad = lax.dot_general(
        attn_input, key_cot, (((0,), (0,)), ((), ())), preferred_element_type=jnp.float32
    )
    cycle_size = lax.axis_size("dp")
    group_size = lax.axis_size("expert")
    shard_rows = key_weight.shape[0]
    stacked = partial_grad.reshape(cycle_size, group_size * shard_rows, partial_grad.shape[1])
    halfway = lax.psum_scatter(stacked.astype(jnp.bfloat16), "dp", scatter_dimension=0, tiled=True)
    summed = lax.psum_scatter(halfway, "expert", scatter_dimension=1, tiled=True).astype(
        jnp.float32
    )
    key_grad = summed.reshape(shard_rows, partial_grad.shape[1])
    new_key_weight, new_first_moment, new_second_moment = adamw(
        key_weight, first_moment, second_moment, key_grad
    )
    return (input_grad, new_key_weight, new_first_moment, new_second_moment)


MESH = pl.DeviceIdType.MESH
CONTRACT_FIRST = (((0,), (0,)), ((), ()))
CONTRACT_LAST = (((1,), (1,)), ((), ()))
SLOTS = 80


def split_columns(values):
    high = values.astype(jnp.bfloat16)
    low = (values - high.astype(jnp.float32)).astype(jnp.bfloat16)
    return jnp.concatenate([high, low], axis=1)


def fused(
    attn_hbm,
    cot_hbm,
    routing_hbm,
    base_hbm,
    router_hbm,
    rows_hbm,
    dots_hbm,
    weight_hbm,
    out_ref,
    grad_ref,
    attn_ref,
    routing_ref,
    base_ref,
    router_ref,
    dots_ref,
    weight_ref,
    rows_own,
    picked,
    blocks,
    info_send,
    info_got,
    dots_send,
    dots_got,
    cots,
    attn_send,
    attn_got,
    window,
    part,
    send,
    relay_got,
    x_got,
    y_got,
    grad_send,
    grad_got,
    local_sem,
    info_ss,
    info_rs,
    rows_ss,
    rows_rs,
    dots_ss,
    dots_rs,
    cot_ss,
    cot_rs,
    twin_ss,
    twin_rs,
    attn_ss,
    attn_rs,
    wz_ss,
    wz_rs,
    wt_ss,
    wt_rs,
    part_ss,
    part_rs,
    gz_ss,
    gz_rs,
):
    tokens, features = out_ref.shape
    experts, capacity = dots_ref.shape
    shard, keys = weight_ref.shape
    layers = window.shape[0]
    slab = features // layers
    half = features // 2
    z, e = lax.axis_index("dp"), lax.axis_index("expert")
    y, x, c = e // 4, (e // 2) % 2, e % 2
    chip = e // 2

    def peer(r):
        return ((y + r // 4) % 2) * 4 + ((x + (r // 2) % 2) % 2) * 2 + (c + r % 2) % 2

    def columns(start, size):
        return pl.ds(pl.multiple_of(start, 128), size)

    def remote(src, dst, send_sem, recv_sem, to):
        copy = pltpu.make_async_remote_copy(
            src_ref=src,
            dst_ref=dst,
            send_sem=send_sem,
            recv_sem=recv_sem,
            device_id=to,
            device_id_type=MESH,
        )
        copy.start()
        return copy

    barrier = pltpu.get_barrier_semaphore()
    for r in range(1, experts):
        pl.semaphore_signal(barrier, inc=1, device_id=(z, peer(r)), device_id_type=MESH)
    for rz in range(1, layers):
        pl.semaphore_signal(
            barrier, inc=1, device_id=((z + rz) % layers, e), device_id_type=MESH
        )
    loads = [
        pltpu.make_async_copy(src, dst, local_sem.at[i])
        for i, (src, dst) in enumerate(
            (
                (routing_hbm, routing_ref),
                (base_hbm, base_ref),
                (weight_hbm, weight_ref),
                (dots_hbm, dots_ref),
                (cot_hbm, cots.at[0]),
                (attn_hbm, attn_ref),
                (rows_hbm, rows_own),
                (router_hbm, router_ref),
            )
        )
    ]
    for load in loads:
        load.start()

    shift = 64 * (chip % 2)

    def window_rows(core):
        return pl.ds(pl.multiple_of(shift + core * shard, 32), shard)

    for load in loads[:4]:
        load.wait()
    window[z, window_rows(c), :] = weight_ref[...].astype(jnp.bfloat16)
    spare = pl.ds(pl.multiple_of(2 * shard * (1 - chip % 2), 64), 64)
    for i in range(layers):
        window[i, spare, :] = jnp.zeros((64, keys), jnp.bfloat16)

    routing = routing_ref[...]
    names = lax.broadcasted_iota(jnp.int32, (experts, tokens), 0)
    choose = jnp.zeros((experts, tokens), jnp.float32)
    for k in range(routing.shape[0]):
        choose = choose + (routing[k : k + 1, :] == names).astype(jnp.float32)
    earlier = (
        lax.broadcasted_iota(jnp.int32, (tokens, tokens), 0)
        < lax.broadcasted_iota(jnp.int32, (tokens, tokens), 1)
    ).astype(jnp.bfloat16)
    before = jnp.dot(choose.astype(jnp.bfloat16), earlier, preferred_element_type=jnp.float32)
    place = jnp.where(choose > 0.0, before, -1.0)
    logits = base_ref[...] + routed_offset * choose
    raised = jnp.exp(logits - jnp.max(logits, axis=0, keepdims=True))
    probs = raised / jnp.sum(raised, axis=0, keepdims=True)
    chosen = probs * choose
    chosen_sum = jnp.sum(chosen, axis=0, keepdims=True)
    gate = chosen / chosen_sum
    info_send[0] = place
    info_send[1] = gate

    dots_all = dots_ref[...].astype(jnp.float32)
    dots_send[...] = jnp.zeros_like(dots_send)
    for j in range(experts):
        dots_send[j, :, 0:capacity] = jnp.broadcast_to(dots_all[j : j + 1, :], (8, capacity))
    loads[5].wait()
    for j in range(experts):
        attn_send[j] = jnp.concatenate(
            [
                attn_ref[:, i * slab + j * shard : i * slab + (j + 1) * shard]
                for i in range(layers)
            ],
            axis=1,
        )
    attn_got[0] = attn_send[e]
    loads[4].wait()
    pl.semaphore_wait(barrier, experts - 1 + layers - 1)

    twin = (z, peer(1))
    info, cot, attn, dots, rows = {}, {}, {}, {}, {}
    for q in (3, 1, 2):
        info[q] = remote(
            info_send, info_got.at[q], info_ss.at[q], info_rs.at[q], (z, peer(2 * q))
        )
    mine = window.at[z, window_rows(c)]
    along = [
        remote(mine, mine, wz_ss.at[rz], wz_rs.at[rz], ((z + rz) % layers, e))
        for rz in range(1, layers)
    ]
    for q in (3, 1, 2):
        cot[q] = remote(
            cots.at[0], cots.at[2 * q], cot_ss.at[q], cot_rs.at[q], (z, peer(2 * q))
        )
    for r in (6, 7, 2, 3, 4, 5, 1):
        attn[r] = remote(
            attn_send.at[peer(r)], attn_got.at[r], attn_ss.at[r], attn_rs.at[r], (z, peer(r))
        )
        dots[r] = remote(
            dots_send.at[peer(r)], dots_got.at[r], dots_ss.at[r], dots_rs.at[r], (z, peer(r))
        )

    loads[6].wait()
    cell = lax.broadcasted_iota(jnp.int32, (SLOTS, experts * capacity), 1)
    first_cell = experts * lax.broadcasted_iota(jnp.int32, (SLOTS, experts * capacity), 0)

    def pick_rows(group):
        pick = jnp.concatenate(
            [
                (cell == first_cell + peer(r)).astype(jnp.float32).astype(jnp.bfloat16)
                for q in group
                for r in (2 * q + 1, 2 * q)
            ],
            axis=0,
        )

        def tile(i, _):
            here = columns(i * slab, slab)
            got = jnp.dot(pick, rows_own[:, here], preferred_element_type=jnp.float32)
            got = got.astype(jnp.bfloat16)
            for k, q in enumerate(group):
                picked[q, :, here] = got[2 * k * SLOTS : (2 * k + 1) * SLOTS]
                blocks[q, 0:SLOTS, here] = got[(2 * k + 1) * SLOTS : (2 * k + 2) * SLOTS]
            return 0

        lax.fori_loop(0, layers, tile, 0)
        for q in group:
            rows[q] = remote(
                picked.at[q],
                blocks.at[q, pl.ds(SLOTS, SLOTS)],
                rows_ss.at[q],
                rows_rs.at[q],
                twin,
            )

    pick_rows((3,))
    pick_rows((1, 2, 0))

    for copy in along:
        copy.wait_recv()
    column = window.at[:, window_rows(c)]
    swap = remote(column, column, wt_ss, wt_rs, twin)
    forward = {0: remote(cots.at[0], cots.at[1], twin_ss.at[0], twin_rs.at[0], twin)}

    slots = lax.broadcasted_iota(jnp.int32, (SLOTS, tokens), 0)

    def row_of(values, expert):
        return jnp.sum(jnp.where(names == expert, values, 0.0), axis=0, keepdims=True)

    def add_rows(q):
        if q:
            info[q].wait_recv()
            place_q, gate_q = info_got[q, 0], info_got[q, 1]
        else:
            place_q, gate_q = place, gate
        share = jnp.concatenate(
            [
                jnp.where(
                    slots == row_of(place_q, expert).astype(jnp.int32),
                    row_of(gate_q, expert),
                    0.0,
                )
                for expert in (e, peer(1))
            ],
            axis=0,
        )
        share = split_columns(share)
        rows[q].wait_recv()

        def tile(i, _):
            here = columns(i * slab, slab)
            both = lax.dot_general(
                share, blocks[q, :, here], CONTRACT_FIRST, preferred_element_type=jnp.float32
            )
            part[q, :, here] = both[:tokens] + both[tokens:]
            return 0

        lax.fori_loop(0, layers, tile, 0)

    start = (chip * 2 * shard) // 128 * 128
    width = window.shape[1]

    def add_key(q):
        def tile(i, _):
            here = columns(i * slab + start, width)
            part[q, :, here] += lax.dot_general(
                cots[2 * q], window[i], CONTRACT_LAST, preferred_element_type=jnp.float32
            )
            return 0

        lax.fori_loop(0, layers, tile, 0)

    left, right = slice(0, half), slice(half, features)
    to_x, to_y = (z, peer(2)), (z, peer(4))
    parts = []

    def send_part(q, cut, dst, number, to):
        parts.append(
            remote(
                send.at[q, :, pl.ds(cut.start, half)],
                dst.at[:, pl.ds(cut.start, half)],
                part_ss.at[number],
                part_rs.at[number],
                to,
            )
        )

    add_rows(3)
    swap.wait_recv()
    cot[3].wait_recv()
    forward[3] = remote(cots.at[6], cots.at[7], twin_ss.at[3], twin_rs.at[3], twin)
    add_key(3)
    send[3] = part[3].astype(jnp.bfloat16)
    send_part(3, left, relay_got, 0, to_x)
    send_part(3, right, relay_got, 1, to_y)
    for q, cut, dst, to in ((1, left, x_got, to_x), (2, right, y_got, to_y)):
        add_rows(q)
        cot[q].wait_recv()
        forward[q] = remote(
            cots.at[2 * q], cots.at[2 * q + 1], twin_ss.at[q], twin_rs.at[q], twin
        )
        add_key(q)
        send[q, :, cut] = part[q, :, cut].astype(jnp.bfloat16)
        send_part(q, cut, dst, q + 1, to)

    for q in range(4):
        forward[q].wait_recv()
    for r in range(1, experts):
        attn[r].wait_recv()
    grad = lax.dot_general(
        attn_got[...].reshape(experts * tokens, layers * shard),
        cots[...].reshape(experts * tokens, keys),
        CONTRACT_FIRST,
        preferred_element_type=jnp.float32,
    )
    grad_send[...] = grad.reshape(layers, shard, keys).astype(jnp.bfloat16)
    outward = {}
    for rz in (2, 1, 3):
        to = (z + rz) % layers
        outward[rz] = remote(
            grad_send.at[to], grad_got.at[rz], gz_ss.at[rz], gz_rs.at[rz], (to, e)
        )
    layer = lax.broadcasted_iota(jnp.int32, (layers, 1, 1), 0)
    grad_ref[...] = jnp.sum(
        jnp.where(layer == z, grad.reshape(layers, shard, keys), 0.0), axis=0
    )

    inner = jnp.zeros((experts, tokens), jnp.float32)
    for r in range(experts):
        if r > 0:
            dots[r].wait_recv()
            got = dots_got[r, :, 0:SLOTS]
        else:
            got = dots_send[e, :, 0:SLOTS]
        expert = peer(r)
        hit = (slots == row_of(place, expert).astype(jnp.int32)).astype(jnp.float32)
        found = jnp.dot(
            got.astype(jnp.bfloat16),
            hit.astype(jnp.bfloat16),
            preferred_element_type=jnp.float32,
        )
        inner = inner + jnp.where(names == expert, found[0:1, :], 0.0)
    mean_inner = jnp.sum(gate * inner, axis=0, keepdims=True)
    d_probs = choose * (inner - mean_inner) / chosen_sum
    d_logits = probs * (d_probs - jnp.sum(probs * d_probs, axis=0, keepdims=True))
    d_parts = split_columns(d_logits)

    add_rows(0)
    add_key(0)

    loads[7].wait()

    def router_tile(i, _):
        here = columns(i * slab, slab)
        both = lax.dot_general(
            d_parts, router_ref[:, here], CONTRACT_FIRST, preferred_element_type=jnp.float32
        )
        part[0, :, here] += both[:tokens] + both[tokens:]
        return 0

    lax.fori_loop(0, layers, router_tile, 0)

    parts[0].wait_recv()
    send[2, :, left] = (
        part[2, :, left] + relay_got[:, left].astype(jnp.float32)
    ).astype(jnp.bfloat16)
    send_part(2, left, y_got, 4, to_y)
    parts[1].wait_recv()
    send[1, :, right] = (
        part[1, :, right] + relay_got[:, right].astype(jnp.float32)
    ).astype(jnp.bfloat16)
    send_part(1, right, x_got, 5, to_x)

    for rz in range(1, layers):
        outward[rz].wait_recv()
    grad_ref[...] = (
        grad_ref[...]
        + grad_got[1].astype(jnp.float32)
        + grad_got[2].astype(jnp.float32)
        + grad_got[3].astype(jnp.float32)
    )
    for copy in parts[2:]:
        copy.wait_recv()
    out_ref[...] = (
        part[0] + x_got[...].astype(jnp.float32) + y_got[...].astype(jnp.float32)
    ).astype(jnp.bfloat16)

    for group in (info, cot, attn, dots, rows, forward, outward):
        for copy in group.values():
            copy.wait_send()
    for copy in [*along, swap, *parts]:
        copy.wait_send()


def fused_local(
    attn_input,
    key_cot,
    routing,
    router_base,
    router_weight,
    expert_rows,
    expert_dots,
    key_weight,
    first_moment,
    second_moment,
):
    tokens, features = attn_input.shape
    experts, capacity, _ = expert_rows.shape
    shard, keys = key_weight.shape
    layers = lax.axis_size("dp")
    b16, f32 = jnp.bfloat16, jnp.float32
    vmem, anywhere = pl.BlockSpec(memory_space=pltpu.VMEM), pl.BlockSpec(memory_space=pl.ANY)
    dma = pltpu.SemaphoreType.DMA
    input_grad, key_grad = pl.pallas_call(
        fused,
        out_shape=(
            jax.ShapeDtypeStruct((tokens, features), b16),
            jax.ShapeDtypeStruct((shard, keys), f32),
        ),
        in_specs=[anywhere] * 8,
        out_specs=[vmem] * 2,
        scratch_shapes=[
            pltpu.VMEM((tokens, features), b16),
            pltpu.VMEM(routing.shape[::-1], jnp.int32),
            pltpu.VMEM(router_base.shape[::-1], f32),
            pltpu.VMEM(router_weight.shape[::-1], b16),
            pltpu.VMEM(expert_dots.shape, b16),
            pltpu.VMEM((shard, keys), f32),
            pltpu.VMEM((experts * capacity, features), b16),
            pltpu.VMEM((4, SLOTS, features), b16),
            pltpu.VMEM((4, 2 * SLOTS, features), b16),
            pltpu.VMEM((2, experts, tokens), f32),
            pltpu.VMEM((4, 2, experts, tokens), f32),
            pltpu.VMEM((experts, 8, 128), f32),
            pltpu.VMEM((experts, 8, 128), f32),
            pltpu.VMEM((experts, tokens, keys), b16),
            pltpu.VMEM((experts, tokens, layers * shard), b16),
            pltpu.VMEM((experts, tokens, layers * shard), b16),
            pltpu.VMEM((layers, 2 * shard + 64, keys), b16),
            pltpu.VMEM((4, tokens, features), f32),
            pltpu.VMEM((4, tokens, features), b16),
            pltpu.VMEM((tokens, features), b16),
            pltpu.VMEM((tokens, features), b16),
            pltpu.VMEM((tokens, features), b16),
            pltpu.VMEM((layers, shard, keys), b16),
            pltpu.VMEM((layers, shard, keys), b16),
            dma((8,)),
            dma((4,)),
            dma((4,)),
            dma((4,)),
            dma((4,)),
            dma((experts,)),
            dma((experts,)),
            dma((4,)),
            dma((4,)),
            dma((4,)),
            dma((4,)),
            dma((experts,)),
            dma((experts,)),
            dma((layers,)),
            dma((layers,)),
            dma,
            dma,
            dma((6,)),
            dma((6,)),
            dma((layers,)),
            dma((layers,)),
        ],
        compiler_params=pltpu.CompilerParams(
            collective_id=0, has_side_effects=True, vmem_limit_bytes=60 * 1024 * 1024
        ),
        cost_estimate=pl.CostEstimate(
            flops=6 * 10**9, bytes_accessed=10**7, transcendentals=10**4
        ),
    )(
        attn_input,
        key_cot,
        routing.T,
        router_base.T,
        router_weight.T,
        expert_rows.transpose(1, 0, 2).reshape(capacity * experts, features),
        expert_dots,
        key_weight,
    )
    return (input_grad, *adamw(key_weight, first_moment, second_moment, key_grad))


def solution(mesh):
    fits = mesh.shape["dp"] == 4 and mesh.shape["expert"] == 8
    in_specs = (
        P(("dp", "expert"), None),
        P(("dp", "expert"), None),
        P(("dp", "expert"), None),
        P(("dp", "expert"), None),
        P(),
        P(("dp", "expert"), None, None),
        P(("dp", "expert"), None),
        P(("dp", "expert"), None),
        P(("dp", "expert"), None),
        P(("dp", "expert"), None),
    )
    out_specs = (
        P(("dp", "expert"), None),
        P(("dp", "expert"), None),
        P(("dp", "expert"), None),
        P(("dp", "expert"), None),
    )
    return jax.shard_map(
        fused_local if fits else local, mesh=mesh, in_specs=in_specs, out_specs=out_specs, check_vma=False)
```

```python
import jax
import jax.numpy as jnp
from jax import lax
from jax.experimental import pallas as pl
from jax.experimental.pallas import tpu as pltpu
from jax.sharding import PartitionSpec as P

ADAM_STEP = 10


beta_one = 0.9
beta_two = 0.95
epsilon = 1e-08
learn_rate = 0.005
decay_rate = 0.1
routed_offset = 3.5


def route_slots(routing, experts, capacity):
    choose = (routing[:, :, None] == jnp.arange(experts, dtype=jnp.int32)[None, None, :]).astype(
        jnp.int32
    )
    per_expert = jnp.sum(choose, axis=1)
    before = jnp.cumsum(per_expert, axis=0) - per_expert
    slots = jnp.sum(choose * before[:, None, :], axis=2)
    return (choose, routing * capacity + slots)


def combine(routing, router_base, returned, returned_dots, router_weight):
    experts, capacity, features = returned.shape
    choose, flat_index = route_slots(routing, experts, capacity)
    routed_mask = jnp.sum(choose, axis=1).astype(jnp.float32)
    router_probs = jax.nn.softmax(router_base + routed_offset * routed_mask, axis=-1)
    picked = jnp.take(returned.reshape(experts * capacity, features), flat_index, axis=0)
    inner = jnp.take(returned_dots.reshape(experts * capacity), flat_index, axis=0).astype(
        jnp.float32
    )
    chosen = jnp.take_along_axis(router_probs, routing, axis=1)
    chosen_sum = jnp.sum(chosen, axis=1, keepdims=True)
    gate_share = chosen / chosen_sum
    mixed = gate_share[:, 0:1] * picked[:, 0].astype(jnp.float32)
    for position in range(1, routing.shape[1]):
        mixed = mixed + gate_share[:, position : position + 1] * picked[:, position].astype(
            jnp.float32
        )
    mean_inner = jnp.sum(gate_share * inner, axis=1, keepdims=True)
    d_chosen = (inner - mean_inner) / chosen_sum
    d_probs = jnp.sum(choose.astype(jnp.float32) * d_chosen[:, :, None], axis=1)
    d_logits = router_probs * (d_probs - jnp.sum(router_probs * d_probs, axis=1, keepdims=True))
    router_term = jnp.dot(
        d_logits, router_weight.astype(jnp.float32).T, precision=lax.Precision.HIGHEST
    )
    return mixed + router_term


def adamw(weight, first, second, grad):
    new_first = beta_one * first + (1.0 - beta_one) * grad
    new_second = beta_two * second + (1.0 - beta_two) * grad * grad
    first_hat = new_first / (1.0 - beta_one**ADAM_STEP)
    second_hat = new_second / (1.0 - beta_two**ADAM_STEP)
    new_weight = weight - learn_rate * (
        first_hat / (jnp.sqrt(second_hat) + epsilon) + decay_rate * weight
    )
    return (new_weight, new_first, new_second)


def local(
    attn_input,
    key_cot,
    routing,
    router_base,
    router_weight,
    expert_rows,
    expert_dots,
    key_weight,
    first_moment,
    second_moment,
):
    returned, returned_dots = (
        lax.all_to_all(expert_rows, "expert", split_axis=0, concat_axis=0, tiled=True),
        lax.all_to_all(expert_dots, "expert", split_axis=0, concat_axis=0, tiled=True),
    )
    moe_term = combine(routing, router_base, returned, returned_dots, router_weight)
    key_term = lax.dot_general(
        key_cot,
        lax.all_gather(key_weight.astype(jnp.bfloat16), ("dp", "expert"), axis=0, tiled=True),
        (((1,), (1,)), ((), ())),
        preferred_element_type=jnp.float32,
    )
    input_grad = (moe_term + key_term).astype(jnp.bfloat16)
    partial_grad = lax.dot_general(
        attn_input, key_cot, (((0,), (0,)), ((), ())), preferred_element_type=jnp.float32
    )
    cycle_size = lax.axis_size("dp")
    group_size = lax.axis_size("expert")
    shard_rows = key_weight.shape[0]
    stacked = partial_grad.reshape(cycle_size, group_size * shard_rows, partial_grad.shape[1])
    halfway = lax.psum_scatter(stacked.astype(jnp.bfloat16), "dp", scatter_dimension=0, tiled=True)
    summed = lax.psum_scatter(halfway, "expert", scatter_dimension=1, tiled=True).astype(
        jnp.float32
    )
    key_grad = summed.reshape(shard_rows, partial_grad.shape[1])
    new_key_weight, new_first_moment, new_second_moment = adamw(
        key_weight, first_moment, second_moment, key_grad
    )
    return (input_grad, new_key_weight, new_first_moment, new_second_moment)


MESH = pl.DeviceIdType.MESH
CONTRACT_FIRST = (((0,), (0,)), ((), ()))
CONTRACT_LAST = (((1,), (1,)), ((), ()))
SLOTS = 80


def split_columns(values):
    high = values.astype(jnp.bfloat16)
    low = (values - high.astype(jnp.float32)).astype(jnp.bfloat16)
    return jnp.concatenate([high, low], axis=1)


def fused(
    attn_hbm,
    cot_hbm,
    routing_hbm,
    base_hbm,
    router_hbm,
    rows_hbm,
    dots_hbm,
    weight_hbm,
    out_ref,
    grad_ref,
    attn_ref,
    routing_ref,
    base_ref,
    router_ref,
    dots_ref,
    weight_ref,
    rows_own,
    picked,
    blocks,
    info_send,
    info_got,
    dots_send,
    dots_got,
    cots,
    attn_send,
    attn_got,
    window,
    part,
    send,
    relay_got,
    x_got,
    y_got,
    grad_own,
    grad_send,
    grad_got,
    cross_send,
    cross_got,
    local_sem,
    info_ss,
    info_rs,
    rows_ss,
    rows_rs,
    dots_ss,
    dots_rs,
    cot_ss,
    cot_rs,
    twin_ss,
    twin_rs,
    attn_ss,
    attn_rs,
    wz_ss,
    wz_rs,
    wt_ss,
    wt_rs,
    part_ss,
    part_rs,
    gz_ss,
    gz_rs,
    gx_ss,
    gx_rs,
):
    tokens, features = out_ref.shape
    experts, capacity = dots_ref.shape
    shard, keys = weight_ref.shape
    layers = window.shape[0]
    slab = features // layers
    half = features // 2
    z, e = lax.axis_index("dp"), lax.axis_index("expert")
    y, x, c = e // 4, (e // 2) % 2, e % 2
    chip = e // 2

    def peer(r):
        return ((y + r // 4) % 2) * 4 + ((x + (r // 2) % 2) % 2) * 2 + (c + r % 2) % 2

    def columns(start, size):
        return pl.ds(pl.multiple_of(start, 128), size)

    def remote(src, dst, send_sem, recv_sem, to):
        copy = pltpu.make_async_remote_copy(
            src_ref=src,
            dst_ref=dst,
            send_sem=send_sem,
            recv_sem=recv_sem,
            device_id=to,
            device_id_type=MESH,
        )
        copy.start()
        return copy

    barrier = pltpu.get_barrier_semaphore()
    for r in range(1, experts):
        pl.semaphore_signal(barrier, inc=1, device_id=(z, peer(r)), device_id_type=MESH)
    for rz in range(1, layers):
        pl.semaphore_signal(
            barrier, inc=1, device_id=((z + rz) % layers, e), device_id_type=MESH
        )
    loads = [
        pltpu.make_async_copy(src, dst, local_sem.at[i])
        for i, (src, dst) in enumerate(
            (
                (routing_hbm, routing_ref),
                (base_hbm, base_ref),
                (weight_hbm, weight_ref),
                (dots_hbm, dots_ref),
                (cot_hbm, cots.at[0]),
                (attn_hbm, attn_ref),
                (rows_hbm, rows_own),
                (router_hbm, router_ref),
            )
        )
    ]
    for load in loads:
        load.start()

    shift = 64 * (chip % 2)

    def window_rows(core):
        return pl.ds(pl.multiple_of(shift + core * shard, 32), shard)

    for load in loads[:4]:
        load.wait()
    window[z, window_rows(c), :] = weight_ref[...].astype(jnp.bfloat16)
    spare = pl.ds(pl.multiple_of(2 * shard * (1 - chip % 2), 64), 64)
    for i in range(layers):
        window[i, spare, :] = jnp.zeros((64, keys), jnp.bfloat16)

    routing = routing_ref[...]
    names = lax.broadcasted_iota(jnp.int32, (experts, tokens), 0)
    choose = jnp.zeros((experts, tokens), jnp.float32)
    for k in range(routing.shape[0]):
        choose = choose + (routing[k : k + 1, :] == names).astype(jnp.float32)
    earlier = (
        lax.broadcasted_iota(jnp.int32, (tokens, tokens), 0)
        < lax.broadcasted_iota(jnp.int32, (tokens, tokens), 1)
    ).astype(jnp.bfloat16)
    before = jnp.dot(choose.astype(jnp.bfloat16), earlier, preferred_element_type=jnp.float32)
    place = jnp.where(choose > 0.0, before, -1.0)
    logits = base_ref[...] + routed_offset * choose
    raised = jnp.exp(logits - jnp.max(logits, axis=0, keepdims=True))
    probs = raised / jnp.sum(raised, axis=0, keepdims=True)
    chosen = probs * choose
    chosen_sum = jnp.sum(chosen, axis=0, keepdims=True)
    gate = chosen / chosen_sum
    info_send[0] = place
    info_send[1] = gate

    dots_all = dots_ref[...].astype(jnp.float32)
    dots_send[...] = jnp.zeros_like(dots_send)
    for j in range(experts):
        dots_send[j, :, 0:capacity] = jnp.broadcast_to(dots_all[j : j + 1, :], (8, capacity))
    loads[5].wait()
    bit = shard // 2
    for across in range(2):
        for near in range(2):
            for core in range(2):
                starts = [
                    i * slab
                    + (near * (4, 2)[1 - across] + far * (4, 2)[across] + core) * shard
                    + across * bit
                    for i in range(layers)
                    for far in range(2)
                ]
                attn_send[across, near * 2 + core] = jnp.concatenate(
                    [attn_ref[:, start : start + bit] for start in starts], axis=1
                )
    attn_got[0, 0] = attn_send[0, x * 2 + c]
    attn_got[1, 0] = attn_send[1, y * 2 + c]
    loads[4].wait()
    pl.semaphore_wait(barrier, experts - 1 + layers - 1)

    twin = (z, peer(1))
    info, cot, attn, dots, rows = {}, {}, {}, {}, {}
    for q in (3, 1, 2):
        info[q] = remote(
            info_send, info_got.at[q], info_ss.at[q], info_rs.at[q], (z, peer(2 * q))
        )
    mine = window.at[z, window_rows(c)]
    along = [
        remote(mine, mine, wz_ss.at[rz], wz_rs.at[rz], ((z + rz) % layers, e))
        for rz in range(1, layers)
    ]
    for q in (3, 1, 2):
        cot[q] = remote(
            cots.at[0], cots.at[2 * q], cot_ss.at[q], cot_rs.at[q], (z, peer(2 * q))
        )
    for across, place_to, r in ((0, 2, 2), (1, 2, 4), (0, 3, 3), (1, 3, 5), (0, 1, 1), (1, 1, 1)):
        to, number = peer(r), across * 4 + place_to
        near = (to // 2) % 2 if across == 0 else to // 4
        attn[number] = remote(
            attn_send.at[across, near * 2 + to % 2],
            attn_got.at[across, place_to],
            attn_ss.at[number],
            attn_rs.at[number],
            (z, to),
        )
    for r in range(1, experts):
        dots[r] = remote(
            dots_send.at[peer(r)], dots_got.at[r], dots_ss.at[r], dots_rs.at[r], (z, peer(r))
        )

    loads[6].wait()
    cell = lax.broadcasted_iota(jnp.int32, (SLOTS, experts * capacity), 1)
    first_cell = experts * lax.broadcasted_iota(jnp.int32, (SLOTS, experts * capacity), 0)

    def pick_rows(group):
        pick = jnp.concatenate(
            [
                (cell == first_cell + peer(r)).astype(jnp.float32).astype(jnp.bfloat16)
                for q in group
                for r in (2 * q + 1, 2 * q)
            ],
            axis=0,
        )

        def tile(i, _):
            here = columns(i * slab, slab)
            got = jnp.dot(pick, rows_own[:, here], preferred_element_type=jnp.float32)
            got = got.astype(jnp.bfloat16)
            for k, q in enumerate(group):
                picked[q, :, here] = got[2 * k * SLOTS : (2 * k + 1) * SLOTS]
                blocks[q, 0:SLOTS, here] = got[(2 * k + 1) * SLOTS : (2 * k + 2) * SLOTS]
            return 0

        lax.fori_loop(0, layers, tile, 0)
        for q in group:
            rows[q] = remote(
                picked.at[q],
                blocks.at[q, pl.ds(SLOTS, SLOTS)],
                rows_ss.at[q],
                rows_rs.at[q],
                twin,
            )

    pick_rows((3,))
    pick_rows((1, 2, 0))

    for copy in along:
        copy.wait_recv()
    column = window.at[:, window_rows(c)]
    swap = remote(column, column, wt_ss, wt_rs, twin)
    forward = {0: remote(cots.at[0], cots.at[1], twin_ss.at[0], twin_rs.at[0], twin)}

    slots = lax.broadcasted_iota(jnp.int32, (SLOTS, tokens), 0)

    def row_of(values, expert):
        return jnp.sum(jnp.where(names == expert, values, 0.0), axis=0, keepdims=True)

    def add_rows(q):
        if q:
            info[q].wait_recv()
            place_q, gate_q = info_got[q, 0], info_got[q, 1]
        else:
            place_q, gate_q = place, gate
        share = jnp.concatenate(
            [
                jnp.where(
                    slots == row_of(place_q, expert).astype(jnp.int32),
                    row_of(gate_q, expert),
                    0.0,
                )
                for expert in (e, peer(1))
            ],
            axis=0,
        )
        share = split_columns(share)
        rows[q].wait_recv()

        def tile(i, _):
            here = columns(i * slab, slab)
            both = lax.dot_general(
                share, blocks[q, :, here], CONTRACT_FIRST, preferred_element_type=jnp.float32
            )
            part[q, :, here] = both[:tokens] + both[tokens:]
            return 0

        lax.fori_loop(0, layers, tile, 0)

    start = (chip * 2 * shard) // 128 * 128
    width = window.shape[1]

    def add_key(q):
        def tile(i, _):
            here = columns(i * slab + start, width)
            part[q, :, here] += lax.dot_general(
                cots[2 * q], window[i], CONTRACT_LAST, preferred_element_type=jnp.float32
            )
            return 0

        lax.fori_loop(0, layers, tile, 0)

    left, right = slice(0, half), slice(half, features)
    to_x, to_y = (z, peer(2)), (z, peer(4))
    parts = []

    def send_part(q, cut, dst, number, to):
        parts.append(
            remote(
                send.at[q, :, pl.ds(cut.start, half)],
                dst.at[:, pl.ds(cut.start, half)],
                part_ss.at[number],
                part_rs.at[number],
                to,
            )
        )

    add_rows(3)
    swap.wait_recv()
    cot[3].wait_recv()
    add_key(3)
    send[3] = part[3].astype(jnp.bfloat16)
    send_part(3, left, relay_got, 0, to_x)
    send_part(3, right, relay_got, 1, to_y)
    for q in (1, 2):
        cot[q].wait_recv()
        forward[q] = remote(
            cots.at[2 * q], cots.at[2 * q + 1], twin_ss.at[q], twin_rs.at[q], twin
        )
    for copy in [*forward.values(), *attn.values()]:
        copy.wait_recv()
    for across in range(2):
        near_cots = jnp.concatenate([cots[0:2], cots[2 + 2 * across : 4 + 2 * across]], axis=0)
        grad = lax.dot_general(
            attn_got[across].reshape(4 * tokens, layers * shard),
            near_cots.reshape(4 * tokens, keys),
            CONTRACT_FIRST,
            preferred_element_type=jnp.float32,
        ).reshape(layers, shard, keys)
        grad_own[:, across * shard : (across + 1) * shard, :] = grad
        grad_send[:, across * shard : (across + 1) * shard, :] = grad.astype(jnp.bfloat16)
    outward = {}
    for rz in (2, 1, 3):
        to = (z + rz) % layers
        outward[rz] = remote(
            grad_send.at[to], grad_got.at[rz], gz_ss.at[rz], gz_rs.at[rz], (to, e)
        )
    for q, cut, dst, to in ((1, left, x_got, to_x), (2, right, y_got, to_y)):
        add_rows(q)
        add_key(q)
        send[q, :, cut] = part[q, :, cut].astype(jnp.bfloat16)
        send_part(q, cut, dst, q + 1, to)

    inner = jnp.zeros((experts, tokens), jnp.float32)
    for r in range(experts):
        if r > 0:
            dots[r].wait_recv()
            got = dots_got[r, :, 0:SLOTS]
        else:
            got = dots_send[e, :, 0:SLOTS]
        expert = peer(r)
        hit = (slots == row_of(place, expert).astype(jnp.int32)).astype(jnp.float32)
        found = jnp.dot(
            got.astype(jnp.bfloat16),
            hit.astype(jnp.bfloat16),
            preferred_element_type=jnp.float32,
        )
        inner = inner + jnp.where(names == expert, found[0:1, :], 0.0)
    mean_inner = jnp.sum(gate * inner, axis=0, keepdims=True)
    d_probs = choose * (inner - mean_inner) / chosen_sum
    d_logits = probs * (d_probs - jnp.sum(probs * d_probs, axis=0, keepdims=True))
    d_parts = split_columns(d_logits)

    add_rows(0)
    add_key(0)

    loads[7].wait()

    def router_tile(i, _):
        here = columns(i * slab, slab)
        both = lax.dot_general(
            d_parts, router_ref[:, here], CONTRACT_FIRST, preferred_element_type=jnp.float32
        )
        part[0, :, here] += both[:tokens] + both[tokens:]
        return 0

    lax.fori_loop(0, layers, router_tile, 0)

    parts[0].wait_recv()
    send[2, :, left] = (
        part[2, :, left] + relay_got[:, left].astype(jnp.float32)
    ).astype(jnp.bfloat16)
    send_part(2, left, y_got, 4, to_y)
    parts[1].wait_recv()
    send[1, :, right] = (
        part[1, :, right] + relay_got[:, right].astype(jnp.float32)
    ).astype(jnp.bfloat16)
    send_part(1, right, x_got, 5, to_x)

    for rz in range(1, layers):
        outward[rz].wait_recv()
    grad_own[0] = (
        grad_own[z]
        + grad_got[1].astype(jnp.float32)
        + grad_got[2].astype(jnp.float32)
        + grad_got[3].astype(jnp.float32)
    )
    final = {}
    for across, mine_o, r in ((0, y, 4), (1, x, 2)):
        other = pl.ds(pl.multiple_of(across * shard + (1 - mine_o) * bit, 16), bit)
        cross_send[across] = grad_own[0, other, :].astype(jnp.bfloat16)
        final[across] = remote(
            cross_send.at[across],
            cross_got.at[across],
            gx_ss.at[across],
            gx_rs.at[across],
            (z, peer(r)),
        )
    for across, mine_o in ((0, y), (1, x)):
        final[across].wait_recv()
        kept = pl.ds(pl.multiple_of(across * shard + mine_o * bit, 16), bit)
        grad_ref[across * bit : (across + 1) * bit, :] = grad_own[0, kept, :] + cross_got[
            across
        ].astype(jnp.float32)
    for copy in parts[2:]:
        copy.wait_recv()
    out_ref[...] = (
        part[0] + x_got[...].astype(jnp.float32) + y_got[...].astype(jnp.float32)
    ).astype(jnp.bfloat16)

    for group in (info, cot, attn, dots, rows, forward, outward, final):
        for copy in group.values():
            copy.wait_send()
    for copy in [*along, swap, *parts]:
        copy.wait_send()


def fused_local(
    attn_input,
    key_cot,
    routing,
    router_base,
    router_weight,
    expert_rows,
    expert_dots,
    key_weight,
    first_moment,
    second_moment,
):
    tokens, features = attn_input.shape
    experts, capacity, _ = expert_rows.shape
    shard, keys = key_weight.shape
    layers = lax.axis_size("dp")
    b16, f32 = jnp.bfloat16, jnp.float32
    vmem, anywhere = pl.BlockSpec(memory_space=pltpu.VMEM), pl.BlockSpec(memory_space=pl.ANY)
    dma = pltpu.SemaphoreType.DMA
    input_grad, key_grad = pl.pallas_call(
        fused,
        out_shape=(
            pltpu.VMEM((tokens, features), b16),
            pltpu.VMEM((shard, keys), f32),
        ),
        in_specs=[anywhere] * 8,
        out_specs=[vmem] * 2,
        scratch_shapes=[
            pltpu.VMEM((tokens, features), b16),
            pltpu.VMEM(routing.shape[::-1], jnp.int32),
            pltpu.VMEM(router_base.shape[::-1], f32),
            pltpu.VMEM(router_weight.shape[::-1], b16),
            pltpu.VMEM(expert_dots.shape, b16),
            pltpu.VMEM((shard, keys), f32),
            pltpu.VMEM((experts * capacity, features), b16),
            pltpu.VMEM((4, SLOTS, features), b16),
            pltpu.VMEM((4, 2 * SLOTS, features), b16),
            pltpu.VMEM((2, experts, tokens), f32),
            pltpu.VMEM((4, 2, experts, tokens), f32),
            pltpu.VMEM((experts, 8, 128), f32),
            pltpu.VMEM((experts, 8, 128), f32),
            pltpu.VMEM((experts, tokens, keys), b16),
            pltpu.VMEM((2, 4, tokens, layers * shard), b16),
            pltpu.VMEM((2, 4, tokens, layers * shard), b16),
            pltpu.VMEM((layers, 2 * shard + 64, keys), b16),
            pltpu.VMEM((4, tokens, features), f32),
            pltpu.VMEM((4, tokens, features), b16),
            pltpu.VMEM((tokens, features), b16),
            pltpu.VMEM((tokens, features), b16),
            pltpu.VMEM((tokens, features), b16),
            pltpu.VMEM((layers, 2 * shard, keys), f32),
            pltpu.VMEM((layers, 2 * shard, keys), b16),
            pltpu.VMEM((layers, 2 * shard, keys), b16),
            pltpu.VMEM((2, shard // 2, keys), b16),
            pltpu.VMEM((2, shard // 2, keys), b16),
            dma((8,)),
            dma((4,)),
            dma((4,)),
            dma((4,)),
            dma((4,)),
            dma((experts,)),
            dma((experts,)),
            dma((4,)),
            dma((4,)),
            dma((4,)),
            dma((4,)),
            dma((experts,)),
            dma((experts,)),
            dma((layers,)),
            dma((layers,)),
            dma,
            dma,
            dma((6,)),
            dma((6,)),
            dma((layers,)),
            dma((layers,)),
            dma((2,)),
            dma((2,)),
        ],
        compiler_params=pltpu.CompilerParams(
            collective_id=0, has_side_effects=True, vmem_limit_bytes=60 * 1024 * 1024
        ),
        cost_estimate=pl.CostEstimate(
            flops=6 * 10**9, bytes_accessed=10**7, transcendentals=10**4
        ),
    )(
        attn_input,
        key_cot,
        routing.T,
        router_base.T,
        router_weight.T,
        expert_rows.transpose(1, 0, 2).reshape(capacity * experts, features),
        expert_dots,
        key_weight,
    )
    return (input_grad, *adamw(key_weight, first_moment, second_moment, key_grad))


def solution(mesh):
    fits = mesh.shape["dp"] == 4 and mesh.shape["expert"] == 8
    in_specs = (
        P(("dp", "expert"), None),
        P(("dp", "expert"), None),
        P(("dp", "expert"), None),
        P(("dp", "expert"), None),
        P(),
        P(("dp", "expert"), None, None),
        P(("dp", "expert"), None),
        P(("dp", "expert"), None),
        P(("dp", "expert"), None),
        P(("dp", "expert"), None),
    )
    out_specs = (
        P(("dp", "expert"), None),
        P(("dp", "expert"), None),
        P(("dp", "expert"), None),
        P(("dp", "expert"), None),
    )
    return jax.shard_map(
        fused_local if fits else local, mesh=mesh, in_specs=in_specs, out_specs=out_specs, check_vma=False)
```

```python
import jax
import jax.numpy as jnp
from jax import lax
from jax.experimental import pallas as pl
from jax.experimental.pallas import tpu as pltpu
from jax.sharding import PartitionSpec as P

ADAM_STEP = 10


beta_one = 0.9
beta_two = 0.95
epsilon = 1e-08
learn_rate = 0.005
decay_rate = 0.1
routed_offset = 3.5


def route_slots(routing, experts, capacity):
    choose = (routing[:, :, None] == jnp.arange(experts, dtype=jnp.int32)[None, None, :]).astype(
        jnp.int32
    )
    per_expert = jnp.sum(choose, axis=1)
    before = jnp.cumsum(per_expert, axis=0) - per_expert
    slots = jnp.sum(choose * before[:, None, :], axis=2)
    return (choose, routing * capacity + slots)


def combine(routing, router_base, returned, returned_dots, router_weight):
    experts, capacity, features = returned.shape
    choose, flat_index = route_slots(routing, experts, capacity)
    routed_mask = jnp.sum(choose, axis=1).astype(jnp.float32)
    router_probs = jax.nn.softmax(router_base + routed_offset * routed_mask, axis=-1)
    picked = jnp.take(returned.reshape(experts * capacity, features), flat_index, axis=0)
    inner = jnp.take(returned_dots.reshape(experts * capacity), flat_index, axis=0).astype(
        jnp.float32
    )
    chosen = jnp.take_along_axis(router_probs, routing, axis=1)
    chosen_sum = jnp.sum(chosen, axis=1, keepdims=True)
    gate_share = chosen / chosen_sum
    mixed = gate_share[:, 0:1] * picked[:, 0].astype(jnp.float32)
    for position in range(1, routing.shape[1]):
        mixed = mixed + gate_share[:, position : position + 1] * picked[:, position].astype(
            jnp.float32
        )
    mean_inner = jnp.sum(gate_share * inner, axis=1, keepdims=True)
    d_chosen = (inner - mean_inner) / chosen_sum
    d_probs = jnp.sum(choose.astype(jnp.float32) * d_chosen[:, :, None], axis=1)
    d_logits = router_probs * (d_probs - jnp.sum(router_probs * d_probs, axis=1, keepdims=True))
    router_term = jnp.dot(
        d_logits, router_weight.astype(jnp.float32).T, precision=lax.Precision.HIGHEST
    )
    return mixed + router_term


def adamw(weight, first, second, grad):
    new_first = beta_one * first + (1.0 - beta_one) * grad
    new_second = beta_two * second + (1.0 - beta_two) * grad * grad
    first_hat = new_first / (1.0 - beta_one**ADAM_STEP)
    second_hat = new_second / (1.0 - beta_two**ADAM_STEP)
    new_weight = weight - learn_rate * (
        first_hat / (jnp.sqrt(second_hat) + epsilon) + decay_rate * weight
    )
    return (new_weight, new_first, new_second)


def local(
    attn_input,
    key_cot,
    routing,
    router_base,
    router_weight,
    expert_rows,
    expert_dots,
    key_weight,
    first_moment,
    second_moment,
):
    returned, returned_dots = (
        lax.all_to_all(expert_rows, "expert", split_axis=0, concat_axis=0, tiled=True),
        lax.all_to_all(expert_dots, "expert", split_axis=0, concat_axis=0, tiled=True),
    )
    moe_term = combine(routing, router_base, returned, returned_dots, router_weight)
    key_term = lax.dot_general(
        key_cot,
        lax.all_gather(key_weight.astype(jnp.bfloat16), ("dp", "expert"), axis=0, tiled=True),
        (((1,), (1,)), ((), ())),
        preferred_element_type=jnp.float32,
    )
    input_grad = (moe_term + key_term).astype(jnp.bfloat16)
    partial_grad = lax.dot_general(
        attn_input, key_cot, (((0,), (0,)), ((), ())), preferred_element_type=jnp.float32
    )
    cycle_size = lax.axis_size("dp")
    group_size = lax.axis_size("expert")
    shard_rows = key_weight.shape[0]
    stacked = partial_grad.reshape(cycle_size, group_size * shard_rows, partial_grad.shape[1])
    halfway = lax.psum_scatter(stacked.astype(jnp.bfloat16), "dp", scatter_dimension=0, tiled=True)
    summed = lax.psum_scatter(halfway, "expert", scatter_dimension=1, tiled=True).astype(
        jnp.float32
    )
    key_grad = summed.reshape(shard_rows, partial_grad.shape[1])
    new_key_weight, new_first_moment, new_second_moment = adamw(
        key_weight, first_moment, second_moment, key_grad
    )
    return (input_grad, new_key_weight, new_first_moment, new_second_moment)


MESH = pl.DeviceIdType.MESH
CONTRACT_FIRST = (((0,), (0,)), ((), ()))
CONTRACT_LAST = (((1,), (1,)), ((), ()))
SLOTS = 80


def split_columns(values):
    high = values.astype(jnp.bfloat16)
    low = (values - high.astype(jnp.float32)).astype(jnp.bfloat16)
    return jnp.concatenate([high, low], axis=1)


def fused(
    attn_hbm,
    cot_hbm,
    routing_hbm,
    base_hbm,
    router_hbm,
    rows_hbm,
    dots_hbm,
    weight_hbm,
    out_ref,
    grad_ref,
    attn_ref,
    routing_ref,
    base_ref,
    router_ref,
    dots_ref,
    weight_ref,
    rows_own,
    picked,
    blocks,
    info_send,
    info_got,
    dots_send,
    dots_got,
    cots,
    attn_send,
    attn_got,
    window,
    part,
    send,
    relay_got,
    x_got,
    y_got,
    grad_own,
    grad_send,
    grad_got,
    cross_send,
    cross_got,
    local_sem,
    info_ss,
    info_rs,
    rows_ss,
    rows_rs,
    dots_ss,
    dots_rs,
    cot_ss,
    cot_rs,
    twin_ss,
    twin_rs,
    attn_ss,
    attn_rs,
    wz_ss,
    wz_rs,
    wt_ss,
    wt_rs,
    part_ss,
    part_rs,
    gz_ss,
    gz_rs,
    gx_ss,
    gx_rs,
):
    tokens, features = out_ref.shape
    experts, capacity = dots_ref.shape
    shard, keys = weight_ref.shape
    layers = window.shape[0]
    slab = features // layers
    z, e = lax.axis_index("dp"), lax.axis_index("expert")
    y, x, c = e // 4, (e // 2) % 2, e % 2
    chip = e // 2

    def peer(r):
        return ((y + r // 4) % 2) * 4 + ((x + (r // 2) % 2) % 2) * 2 + (c + r % 2) % 2

    def columns(start, size):
        return pl.ds(pl.multiple_of(start, 128), size)

    def remote(src, dst, send_sem, recv_sem, to):
        copy = pltpu.make_async_remote_copy(
            src_ref=src,
            dst_ref=dst,
            send_sem=send_sem,
            recv_sem=recv_sem,
            device_id=to,
            device_id_type=MESH,
        )
        copy.start()
        return copy

    barrier = pltpu.get_barrier_semaphore()
    for r in range(1, experts):
        pl.semaphore_signal(barrier, inc=1, device_id=(z, peer(r)), device_id_type=MESH)
    for rz in range(1, layers):
        pl.semaphore_signal(
            barrier, inc=1, device_id=((z + rz) % layers, e), device_id_type=MESH
        )
    loads = [
        pltpu.make_async_copy(src, dst, local_sem.at[i])
        for i, (src, dst) in enumerate(
            (
                (routing_hbm, routing_ref),
                (base_hbm, base_ref),
                (weight_hbm, weight_ref),
                (dots_hbm, dots_ref),
                (cot_hbm, cots.at[0]),
                (attn_hbm, attn_ref),
                (rows_hbm, rows_own),
                (router_hbm, router_ref),
            )
        )
    ]
    for load in loads:
        load.start()

    shift = 64 * (chip % 2)

    def window_rows(core):
        return pl.ds(pl.multiple_of(shift + core * shard, 32), shard)

    for load in loads[:4]:
        load.wait()
    window[z, window_rows(c), :] = weight_ref[...].astype(jnp.bfloat16)
    spare = pl.ds(pl.multiple_of(2 * shard * (1 - chip % 2), 64), 64)
    for i in range(layers):
        window[i, spare, :] = jnp.zeros((64, keys), jnp.bfloat16)

    routing = routing_ref[...]
    names = lax.broadcasted_iota(jnp.int32, (experts, tokens), 0)
    choose = jnp.zeros((experts, tokens), jnp.float32)
    for k in range(routing.shape[0]):
        choose = choose + (routing[k : k + 1, :] == names).astype(jnp.float32)
    earlier = (
        lax.broadcasted_iota(jnp.int32, (tokens, tokens), 0)
        < lax.broadcasted_iota(jnp.int32, (tokens, tokens), 1)
    ).astype(jnp.bfloat16)
    before = jnp.dot(choose.astype(jnp.bfloat16), earlier, preferred_element_type=jnp.float32)
    place = jnp.where(choose > 0.0, before, -1.0)
    logits = base_ref[...] + routed_offset * choose
    raised = jnp.exp(logits - jnp.max(logits, axis=0, keepdims=True))
    probs = raised / jnp.sum(raised, axis=0, keepdims=True)
    chosen = probs * choose
    chosen_sum = jnp.sum(chosen, axis=0, keepdims=True)
    gate = chosen / chosen_sum
    info_send[0] = place
    info_send[1] = gate

    dots_all = dots_ref[...].astype(jnp.float32)
    dots_send[...] = jnp.zeros_like(dots_send)
    for j in range(experts):
        dots_send[j, :, 0:capacity] = jnp.broadcast_to(dots_all[j : j + 1, :], (8, capacity))
    loads[4].wait()
    pl.semaphore_wait(barrier, experts - 1 + layers - 1)

    twin = (z, peer(1))
    info, cot, attn, dots, rows = {}, {}, {}, {}, {}
    for q in (3, 1, 2):
        info[q] = remote(
            info_send, info_got.at[q], info_ss.at[q], info_rs.at[q], (z, peer(2 * q))
        )
    mine = window.at[z, window_rows(c)]
    swap = {0: remote(mine, mine, wt_ss.at[0], wt_rs.at[0], twin)}
    along = {
        rz: remote(mine, mine, wz_ss.at[rz], wz_rs.at[rz], ((z + rz) % layers, e))
        for rz in (3, 2, 1)
    }
    for q in (3, 1, 2):
        cot[q] = remote(
            cots.at[0], cots.at[2 * q], cot_ss.at[q], cot_rs.at[q], (z, peer(2 * q))
        )
    forward = {0: remote(cots.at[0], cots.at[1], twin_ss.at[0], twin_rs.at[0], twin)}
    loads[6].wait()
    cell = lax.broadcasted_iota(jnp.int32, (SLOTS, experts * capacity), 1)
    first_cell = experts * lax.broadcasted_iota(jnp.int32, (SLOTS, experts * capacity), 0)

    def pick_rows(group):
        pick = jnp.concatenate(
            [
                (cell == first_cell + peer(r)).astype(jnp.float32).astype(jnp.bfloat16)
                for q in group
                for r in (2 * q + 1, 2 * q)
            ],
            axis=0,
        )

        def tile(i, _):
            here = columns(i * slab, slab)
            got = jnp.dot(pick, rows_own[:, here], preferred_element_type=jnp.float32)
            got = got.astype(jnp.bfloat16)
            for k, q in enumerate(group):
                picked[q, :, here] = got[2 * k * SLOTS : (2 * k + 1) * SLOTS]
                blocks[q, 0:SLOTS, here] = got[(2 * k + 1) * SLOTS : (2 * k + 2) * SLOTS]
            return 0

        lax.fori_loop(0, layers, tile, 0)
        for q in group:
            rows[q] = remote(
                picked.at[q],
                blocks.at[q, pl.ds(SLOTS, SLOTS)],
                rows_ss.at[q],
                rows_rs.at[q],
                twin,
            )

    pick_rows((3,))
    loads[5].wait()
    bit = shard // 2
    for across in range(2):
        for near in range(2):
            for core in range(2):
                starts = [
                    i * slab
                    + (near * (4, 2)[1 - across] + far * (4, 2)[across] + core) * shard
                    + across * bit
                    for i in range(layers)
                    for far in range(2)
                ]
                attn_send[across, near * 2 + core] = jnp.concatenate(
                    [attn_ref[:, start : start + bit] for start in starts], axis=1
                )
    attn_got[0, 0] = attn_send[0, x * 2 + c]
    attn_got[1, 0] = attn_send[1, y * 2 + c]
    for across, place_to, r in ((0, 2, 2), (1, 2, 4), (0, 3, 3), (1, 3, 5), (0, 1, 1), (1, 1, 1)):
        to, number = peer(r), across * 4 + place_to
        near = (to // 2) % 2 if across == 0 else to // 4
        attn[number] = remote(
            attn_send.at[across, near * 2 + to % 2],
            attn_got.at[across, place_to],
            attn_ss.at[number],
            attn_rs.at[number],
            (z, to),
        )
    for r in range(1, experts):
        dots[r] = remote(
            dots_send.at[peer(r)], dots_got.at[r], dots_ss.at[r], dots_rs.at[r], (z, peer(r))
        )

    pick_rows((1, 2))

    def pass_on(k):
        along[layers - k].wait_recv()
        block = window.at[(z + k) % layers, window_rows(c)]
        swap[k] = remote(block, block, wt_ss.at[k], wt_rs.at[k], twin)

    pass_on(1)
    slots = lax.broadcasted_iota(jnp.int32, (SLOTS, tokens), 0)

    def row_of(values, expert):
        return jnp.sum(jnp.where(names == expert, values, 0.0), axis=0, keepdims=True)

    shares = {}

    def make_share(q):
        if q:
            info[q].wait_recv()
            place_q, gate_q = info_got[q, 0], info_got[q, 1]
        else:
            place_q, gate_q = place, gate
        share = jnp.concatenate(
            [
                jnp.where(
                    slots == row_of(place_q, expert).astype(jnp.int32),
                    row_of(gate_q, expert),
                    0.0,
                )
                for expert in (e, peer(1))
            ],
            axis=0,
        )
        shares[q] = split_columns(share)
        rows[q].wait_recv()

    start = (chip * 2 * shard) // 128 * 128
    width = window.shape[1]

    def slab_of(k):
        return columns(((z + k) % layers) * slab, slab)

    def add_rows(q, k):
        here = slab_of(k)
        both = lax.dot_general(
            shares[q], blocks[q, :, here], CONTRACT_FIRST, preferred_element_type=jnp.float32
        )
        part[q, :, here] = both[:tokens] + both[tokens:]

    def add_key(q, k):
        here = columns(((z + k) % layers) * slab + start, width)
        part[q, :, here] += lax.dot_general(
            cots[2 * q],
            window[(z + k) % layers],
            CONTRACT_LAST,
            preferred_element_type=jnp.float32,
        )

    to_x, to_y = (z, peer(2)), (z, peer(4))
    x_first = [(to_x, x_got), (to_y, y_got)]
    relays, direct, onward = {}, {}, {}

    def send_slab(q, k, dst, number, to):
        here = slab_of(k)
        return remote(
            send.at[q, :, here], dst.at[:, here], part_ss.at[number], part_rs.at[number], to
        )

    make_share(3)
    for k in range(layers):
        add_rows(3, k)
    cot[3].wait_recv()
    for k in range(layers):
        swap[k].wait_recv()
        add_key(3, k)
        here = slab_of(k)
        send[3, :, here] = part[3, :, here].astype(jnp.bfloat16)
        relays[k] = send_slab(3, k, relay_got, k, x_first[k % 2][0])
        if k == 0:
            pass_on(2)
            pass_on(3)

    for q in (1, 2):
        cot[q].wait_recv()
        forward[q] = remote(
            cots.at[2 * q], cots.at[2 * q + 1], twin_ss.at[q], twin_rs.at[q], twin
        )
    for copy in [*forward.values(), *attn.values()]:
        copy.wait_recv()
    for across in range(2):
        near_cots = jnp.concatenate([cots[0:2], cots[2 + 2 * across : 4 + 2 * across]], axis=0)
        grad = lax.dot_general(
            attn_got[across].reshape(4 * tokens, layers * shard),
            near_cots.reshape(4 * tokens, keys),
            CONTRACT_FIRST,
            preferred_element_type=jnp.float32,
        ).reshape(layers, shard, keys)
        grad_own[:, across * shard : (across + 1) * shard, :] = grad
        grad_send[:, across * shard : (across + 1) * shard, :] = grad.astype(jnp.bfloat16)
    outward = {}
    for rz in (2, 1, 3):
        to = (z + rz) % layers
        outward[rz] = remote(
            grad_send.at[to], grad_got.at[rz], gz_ss.at[rz], gz_rs.at[rz], (to, e)
        )
    make_share(1)
    make_share(2)
    for k in range(layers):
        q, (to, dst) = k % 2 + 1, x_first[k % 2]
        add_rows(q, k)
        add_key(q, k)
        here = slab_of(k)
        send[q, :, here] = part[q, :, here].astype(jnp.bfloat16)
        direct[k] = send_slab(q, k, dst, layers + k, to)
    for k in range(layers):
        q, (to, dst) = 2 - k % 2, x_first[1 - k % 2]
        add_rows(q, k)
        add_key(q, k)
        relays[k].wait_recv()
        here = slab_of(k)
        send[q, :, here] = (
            part[q, :, here] + relay_got[:, here].astype(jnp.float32)
        ).astype(jnp.bfloat16)
        onward[k] = send_slab(q, k, dst, 2 * layers + k, to)

    pick_rows((0,))
    inner = jnp.zeros((experts, tokens), jnp.float32)
    for r in range(experts):
        if r > 0:
            dots[r].wait_recv()
            got = dots_got[r, :, 0:SLOTS]
        else:
            got = dots_send[e, :, 0:SLOTS]
        expert = peer(r)
        hit = (slots == row_of(place, expert).astype(jnp.int32)).astype(jnp.float32)
        found = jnp.dot(
            got.astype(jnp.bfloat16),
            hit.astype(jnp.bfloat16),
            preferred_element_type=jnp.float32,
        )
        inner = inner + jnp.where(names == expert, found[0:1, :], 0.0)
    mean_inner = jnp.sum(gate * inner, axis=0, keepdims=True)
    d_probs = choose * (inner - mean_inner) / chosen_sum
    d_logits = probs * (d_probs - jnp.sum(probs * d_probs, axis=0, keepdims=True))
    d_parts = split_columns(d_logits)

    make_share(0)
    for k in range(layers):
        add_rows(0, k)
        add_key(0, k)

    loads[7].wait()

    def router_tile(i, _):
        here = columns(i * slab, slab)
        both = lax.dot_general(
            d_parts, router_ref[:, here], CONTRACT_FIRST, preferred_element_type=jnp.float32
        )
        part[0, :, here] += both[:tokens] + both[tokens:]
        return 0

    lax.fori_loop(0, layers, router_tile, 0)

    for rz in range(1, layers):
        outward[rz].wait_recv()
    grad_own[0] = (
        grad_own[z]
        + grad_got[1].astype(jnp.float32)
        + grad_got[2].astype(jnp.float32)
        + grad_got[3].astype(jnp.float32)
    )
    final = {}
    for across, mine_o, r in ((0, y, 4), (1, x, 2)):
        other = pl.ds(pl.multiple_of(across * shard + (1 - mine_o) * bit, 16), bit)
        cross_send[across] = grad_own[0, other, :].astype(jnp.bfloat16)
        final[across] = remote(
            cross_send.at[across],
            cross_got.at[across],
            gx_ss.at[across],
            gx_rs.at[across],
            (z, peer(r)),
        )
    for k in range(layers):
        direct[k].wait_recv()
        onward[k].wait_recv()
        here = slab_of(k)
        out_ref[:, here] = (
            part[0, :, here]
            + x_got[:, here].astype(jnp.float32)
            + y_got[:, here].astype(jnp.float32)
        ).astype(jnp.bfloat16)
    for across, mine_o in ((0, y), (1, x)):
        final[across].wait_recv()
        kept = pl.ds(pl.multiple_of(across * shard + mine_o * bit, 16), bit)
        grad_ref[across * bit : (across + 1) * bit, :] = grad_own[0, kept, :] + cross_got[
            across
        ].astype(jnp.float32)
    for group in (info, cot, attn, dots, rows, forward, outward, final):
        for copy in group.values():
            copy.wait_send()
    for group in (along, swap, relays, direct, onward):
        for copy in group.values():
            copy.wait_send()


def fused_local(
    attn_input,
    key_cot,
    routing,
    router_base,
    router_weight,
    expert_rows,
    expert_dots,
    key_weight,
    first_moment,
    second_moment,
):
    tokens, features = attn_input.shape
    experts, capacity, _ = expert_rows.shape
    shard, keys = key_weight.shape
    layers = lax.axis_size("dp")
    b16, f32 = jnp.bfloat16, jnp.float32
    vmem, anywhere = pl.BlockSpec(memory_space=pltpu.VMEM), pl.BlockSpec(memory_space=pl.ANY)
    dma = pltpu.SemaphoreType.DMA
    input_grad, key_grad = pl.pallas_call(
        fused,
        out_shape=(
            pltpu.VMEM((tokens, features), b16),
            pltpu.VMEM((shard, keys), f32),
        ),
        in_specs=[anywhere] * 8,
        out_specs=[vmem] * 2,
        scratch_shapes=[
            pltpu.VMEM((tokens, features), b16),
            pltpu.VMEM(routing.shape[::-1], jnp.int32),
            pltpu.VMEM(router_base.shape[::-1], f32),
            pltpu.VMEM(router_weight.shape[::-1], b16),
            pltpu.VMEM(expert_dots.shape, b16),
            pltpu.VMEM((shard, keys), f32),
            pltpu.VMEM((experts * capacity, features), b16),
            pltpu.VMEM((4, SLOTS, features), b16),
            pltpu.VMEM((4, 2 * SLOTS, features), b16),
            pltpu.VMEM((2, experts, tokens), f32),
            pltpu.VMEM((4, 2, experts, tokens), f32),
            pltpu.VMEM((experts, 8, 128), f32),
            pltpu.VMEM((experts, 8, 128), f32),
            pltpu.VMEM((experts, tokens, keys), b16),
            pltpu.VMEM((2, 4, tokens, layers * shard), b16),
            pltpu.VMEM((2, 4, tokens, layers * shard), b16),
            pltpu.VMEM((layers, 2 * shard + 64, keys), b16),
            pltpu.VMEM((4, tokens, features), f32),
            pltpu.VMEM((4, tokens, features), b16),
            pltpu.VMEM((tokens, features), b16),
            pltpu.VMEM((tokens, features), b16),
            pltpu.VMEM((tokens, features), b16),
            pltpu.VMEM((layers, 2 * shard, keys), f32),
            pltpu.VMEM((layers, 2 * shard, keys), b16),
            pltpu.VMEM((layers, 2 * shard, keys), b16),
            pltpu.VMEM((2, shard // 2, keys), b16),
            pltpu.VMEM((2, shard // 2, keys), b16),
            dma((8,)),
            dma((4,)),
            dma((4,)),
            dma((4,)),
            dma((4,)),
            dma((experts,)),
            dma((experts,)),
            dma((4,)),
            dma((4,)),
            dma((4,)),
            dma((4,)),
            dma((experts,)),
            dma((experts,)),
            dma((layers,)),
            dma((layers,)),
            dma((layers,)),
            dma((layers,)),
            dma((3 * layers,)),
            dma((3 * layers,)),
            dma((layers,)),
            dma((layers,)),
            dma((2,)),
            dma((2,)),
        ],
        compiler_params=pltpu.CompilerParams(
            collective_id=0, has_side_effects=True, vmem_limit_bytes=60 * 1024 * 1024
        ),
        cost_estimate=pl.CostEstimate(
            flops=6 * 10**9, bytes_accessed=10**7, transcendentals=10**4
        ),
    )(
        attn_input,
        key_cot,
        routing.T,
        router_base.T,
        router_weight.T,
        expert_rows.transpose(1, 0, 2).reshape(capacity * experts, features),
        expert_dots,
        key_weight,
    )
    return (input_grad, *adamw(key_weight, first_moment, second_moment, key_grad))


def solution(mesh):
    fits = mesh.shape["dp"] == 4 and mesh.shape["expert"] == 8
    in_specs = (
        P(("dp", "expert"), None),
        P(("dp", "expert"), None),
        P(("dp", "expert"), None),
        P(("dp", "expert"), None),
        P(),
        P(("dp", "expert"), None, None),
        P(("dp", "expert"), None),
        P(("dp", "expert"), None),
        P(("dp", "expert"), None),
        P(("dp", "expert"), None),
    )
    out_specs = (
        P(("dp", "expert"), None),
        P(("dp", "expert"), None),
        P(("dp", "expert"), None),
        P(("dp", "expert"), None),
    )
    return jax.shard_map(
        fused_local if fits else local, mesh=mesh, in_specs=in_specs, out_specs=out_specs, check_vma=False)
```

```python
import jax
import jax.numpy as jnp
from jax import lax
from jax.experimental import pallas as pl
from jax.experimental.pallas import tpu as pltpu
from jax.sharding import PartitionSpec as P

ADAM_STEP = 10


beta_one = 0.9
beta_two = 0.95
epsilon = 1e-08
learn_rate = 0.005
decay_rate = 0.1
routed_offset = 3.5


def route_slots(routing, experts, capacity):
    choose = (routing[:, :, None] == jnp.arange(experts, dtype=jnp.int32)[None, None, :]).astype(
        jnp.int32
    )
    per_expert = jnp.sum(choose, axis=1)
    before = jnp.cumsum(per_expert, axis=0) - per_expert
    slots = jnp.sum(choose * before[:, None, :], axis=2)
    return (choose, routing * capacity + slots)


def combine(routing, router_base, returned, returned_dots, router_weight):
    experts, capacity, features = returned.shape
    choose, flat_index = route_slots(routing, experts, capacity)
    routed_mask = jnp.sum(choose, axis=1).astype(jnp.float32)
    router_probs = jax.nn.softmax(router_base + routed_offset * routed_mask, axis=-1)
    picked = jnp.take(returned.reshape(experts * capacity, features), flat_index, axis=0)
    inner = jnp.take(returned_dots.reshape(experts * capacity), flat_index, axis=0).astype(
        jnp.float32
    )
    chosen = jnp.take_along_axis(router_probs, routing, axis=1)
    chosen_sum = jnp.sum(chosen, axis=1, keepdims=True)
    gate_share = chosen / chosen_sum
    mixed = gate_share[:, 0:1] * picked[:, 0].astype(jnp.float32)
    for position in range(1, routing.shape[1]):
        mixed = mixed + gate_share[:, position : position + 1] * picked[:, position].astype(
            jnp.float32
        )
    mean_inner = jnp.sum(gate_share * inner, axis=1, keepdims=True)
    d_chosen = (inner - mean_inner) / chosen_sum
    d_probs = jnp.sum(choose.astype(jnp.float32) * d_chosen[:, :, None], axis=1)
    d_logits = router_probs * (d_probs - jnp.sum(router_probs * d_probs, axis=1, keepdims=True))
    router_term = jnp.dot(
        d_logits, router_weight.astype(jnp.float32).T, precision=lax.Precision.HIGHEST
    )
    return mixed + router_term


def adamw(weight, first, second, grad):
    new_first = beta_one * first + (1.0 - beta_one) * grad
    new_second = beta_two * second + (1.0 - beta_two) * grad * grad
    first_hat = new_first / (1.0 - beta_one**ADAM_STEP)
    second_hat = new_second / (1.0 - beta_two**ADAM_STEP)
    new_weight = weight - learn_rate * (
        first_hat / (jnp.sqrt(second_hat) + epsilon) + decay_rate * weight
    )
    return (new_weight, new_first, new_second)


def local(
    attn_input,
    key_cot,
    routing,
    router_base,
    router_weight,
    expert_rows,
    expert_dots,
    key_weight,
    first_moment,
    second_moment,
):
    returned, returned_dots = (
        lax.all_to_all(expert_rows, "expert", split_axis=0, concat_axis=0, tiled=True),
        lax.all_to_all(expert_dots, "expert", split_axis=0, concat_axis=0, tiled=True),
    )
    moe_term = combine(routing, router_base, returned, returned_dots, router_weight)
    key_term = lax.dot_general(
        key_cot,
        lax.all_gather(key_weight.astype(jnp.bfloat16), ("dp", "expert"), axis=0, tiled=True),
        (((1,), (1,)), ((), ())),
        preferred_element_type=jnp.float32,
    )
    input_grad = (moe_term + key_term).astype(jnp.bfloat16)
    partial_grad = lax.dot_general(
        attn_input, key_cot, (((0,), (0,)), ((), ())), preferred_element_type=jnp.float32
    )
    cycle_size = lax.axis_size("dp")
    group_size = lax.axis_size("expert")
    shard_rows = key_weight.shape[0]
    stacked = partial_grad.reshape(cycle_size, group_size * shard_rows, partial_grad.shape[1])
    halfway = lax.psum_scatter(stacked.astype(jnp.bfloat16), "dp", scatter_dimension=0, tiled=True)
    summed = lax.psum_scatter(halfway, "expert", scatter_dimension=1, tiled=True).astype(
        jnp.float32
    )
    key_grad = summed.reshape(shard_rows, partial_grad.shape[1])
    new_key_weight, new_first_moment, new_second_moment = adamw(
        key_weight, first_moment, second_moment, key_grad
    )
    return (input_grad, new_key_weight, new_first_moment, new_second_moment)


MESH = pl.DeviceIdType.MESH
CONTRACT_FIRST = (((0,), (0,)), ((), ()))
CONTRACT_LAST = (((1,), (1,)), ((), ()))
SLOTS = 80


def split_columns(values):
    high = values.astype(jnp.bfloat16)
    low = (values - high.astype(jnp.float32)).astype(jnp.bfloat16)
    return jnp.concatenate([high, low], axis=1)


def fused(
    attn_hbm,
    cot_hbm,
    routing_hbm,
    base_hbm,
    router_hbm,
    rows_hbm,
    dots_hbm,
    weight_hbm,
    out_ref,
    grad_ref,
    attn_ref,
    routing_ref,
    base_ref,
    router_ref,
    dots_ref,
    weight_ref,
    rows_own,
    picked,
    blocks,
    info_send,
    info_got,
    dots_send,
    dots_got,
    cots,
    attn_send,
    attn_got,
    window,
    part,
    send,
    relay_got,
    x_got,
    y_got,
    grad_own,
    grad_send,
    grad_got,
    cross_send,
    cross_got,
    local_sem,
    info_ss,
    info_rs,
    rows_ss,
    rows_rs,
    dots_ss,
    dots_rs,
    cot_ss,
    cot_rs,
    twin_ss,
    twin_rs,
    attn_ss,
    attn_rs,
    wz_ss,
    wz_rs,
    wt_ss,
    wt_rs,
    part_ss,
    part_rs,
    gz_ss,
    gz_rs,
    gx_ss,
    gx_rs,
):
    tokens, features = out_ref.shape
    experts, capacity = dots_ref.shape
    shard, keys = weight_ref.shape
    layers = window.shape[0]
    slab = features // layers
    z, e = lax.axis_index("dp"), lax.axis_index("expert")
    y, x, c = e // 4, (e // 2) % 2, e % 2
    chip = e // 2

    def peer(r):
        return ((y + r // 4) % 2) * 4 + ((x + (r // 2) % 2) % 2) * 2 + (c + r % 2) % 2

    def columns(start, size):
        return pl.ds(pl.multiple_of(start, 128), size)

    def remote(src, dst, send_sem, recv_sem, to):
        copy = pltpu.make_async_remote_copy(
            src_ref=src,
            dst_ref=dst,
            send_sem=send_sem,
            recv_sem=recv_sem,
            device_id=to,
            device_id_type=MESH,
        )
        copy.start()
        return copy

    barrier = pltpu.get_barrier_semaphore()
    for r in range(1, experts):
        pl.semaphore_signal(barrier, inc=1, device_id=(z, peer(r)), device_id_type=MESH)
    for rz in range(1, layers):
        pl.semaphore_signal(
            barrier, inc=1, device_id=((z + rz) % layers, e), device_id_type=MESH
        )
    loads = [
        pltpu.make_async_copy(src, dst, local_sem.at[i])
        for i, (src, dst) in enumerate(
            (
                (routing_hbm, routing_ref),
                (base_hbm, base_ref),
                (weight_hbm, weight_ref),
                (dots_hbm, dots_ref),
                (cot_hbm, cots.at[0]),
                (attn_hbm, attn_ref),
                (rows_hbm, rows_own),
                (router_hbm, router_ref),
            )
        )
    ]
    for load in loads:
        load.start()

    shift = 64 * (chip % 2)

    def window_rows(core):
        return pl.ds(pl.multiple_of(shift + core * shard, 32), shard)

    loads[2].wait()
    window[z, window_rows(c), :] = weight_ref[...].astype(jnp.bfloat16)
    spare = pl.ds(pl.multiple_of(2 * shard * (1 - chip % 2), 64), 64)
    for i in range(layers):
        window[i, spare, :] = jnp.zeros((64, keys), jnp.bfloat16)

    loads[4].wait()
    pl.semaphore_wait(barrier, experts - 1 + layers - 1)

    twin = (z, peer(1))
    info, cot, attn, dots, rows = {}, {}, {}, {}, {}
    mine = window.at[z, window_rows(c)]
    swap = {0: remote(mine, mine, wt_ss.at[0], wt_rs.at[0], twin)}
    along = {
        rz: remote(mine, mine, wz_ss.at[rz], wz_rs.at[rz], ((z + rz) % layers, e))
        for rz in (3, 2, 1)
    }
    for q in (1, 2):
        cot[q] = remote(
            cots.at[0], cots.at[2 * q], cot_ss.at[q], cot_rs.at[q], (z, peer(2 * q))
        )
    forward = {0: remote(cots.at[0], cots.at[1], twin_ss.at[0], twin_rs.at[0], twin)}
    for i in (0, 1, 3):
        loads[i].wait()
    routing = routing_ref[...]
    names = lax.broadcasted_iota(jnp.int32, (experts, tokens), 0)
    choose = jnp.zeros((experts, tokens), jnp.float32)
    for k in range(routing.shape[0]):
        choose = choose + (routing[k : k + 1, :] == names).astype(jnp.float32)
    earlier = (
        lax.broadcasted_iota(jnp.int32, (tokens, tokens), 0)
        < lax.broadcasted_iota(jnp.int32, (tokens, tokens), 1)
    ).astype(jnp.bfloat16)
    before = jnp.dot(choose.astype(jnp.bfloat16), earlier, preferred_element_type=jnp.float32)
    place = jnp.where(choose > 0.0, before, -1.0)
    logits = base_ref[...] + routed_offset * choose
    raised = jnp.exp(logits - jnp.max(logits, axis=0, keepdims=True))
    probs = raised / jnp.sum(raised, axis=0, keepdims=True)
    chosen = probs * choose
    chosen_sum = jnp.sum(chosen, axis=0, keepdims=True)
    gate = chosen / chosen_sum
    info_send[0] = place
    info_send[1] = gate

    dots_all = dots_ref[...].astype(jnp.float32)
    dots_send[...] = jnp.zeros_like(dots_send)
    for j in range(experts):
        dots_send[j, :, 0:capacity] = jnp.broadcast_to(dots_all[j : j + 1, :], (8, capacity))
    for q in (3, 1, 2):
        info[q] = remote(
            info_send, info_got.at[q], info_ss.at[q], info_rs.at[q], (z, peer(2 * q))
        )
    loads[6].wait()
    cell = lax.broadcasted_iota(jnp.int32, (SLOTS, experts * capacity), 1)
    first_cell = experts * lax.broadcasted_iota(jnp.int32, (SLOTS, experts * capacity), 0)

    def pick_rows(group):
        pick = jnp.concatenate(
            [
                (cell == first_cell + peer(r)).astype(jnp.float32).astype(jnp.bfloat16)
                for q in group
                for r in (2 * q + 1, 2 * q)
            ],
            axis=0,
        )

        def tile(i, _):
            here = columns(i * slab, slab)
            got = jnp.dot(pick, rows_own[:, here], preferred_element_type=jnp.float32)
            got = got.astype(jnp.bfloat16)
            for k, q in enumerate(group):
                picked[q, :, here] = got[2 * k * SLOTS : (2 * k + 1) * SLOTS]
                blocks[q, 0:SLOTS, here] = got[(2 * k + 1) * SLOTS : (2 * k + 2) * SLOTS]
            return 0

        lax.fori_loop(0, layers, tile, 0)
        for q in group:
            rows[q] = remote(
                picked.at[q],
                blocks.at[q, pl.ds(SLOTS, SLOTS)],
                rows_ss.at[q],
                rows_rs.at[q],
                twin,
            )

    pick_rows((3,))
    for q in (1, 2):
        cot[q].wait_recv()
        piece = pl.ds((q - 1) * (tokens // 2), tokens // 2)
        cot[2 + q] = remote(
            cots.at[2 * q, piece],
            cots.at[6, piece],
            cot_ss.at[2 + q],
            cot_rs.at[2 + q],
            (z, peer(6 - 2 * q)),
        )
        forward[q] = remote(
            cots.at[2 * q], cots.at[2 * q + 1], twin_ss.at[q], twin_rs.at[q], twin
        )
    loads[5].wait()
    bit = shard // 2
    for across in range(2):
        for near in range(2):
            for core in range(2):
                starts = [
                    i * slab
                    + (near * (4, 2)[1 - across] + far * (4, 2)[across] + core) * shard
                    + across * bit
                    for i in range(layers)
                    for far in range(2)
                ]
                attn_send[across, near * 2 + core] = jnp.concatenate(
                    [attn_ref[:, start : start + bit] for start in starts], axis=1
                )
    attn_got[0, 0] = attn_send[0, x * 2 + c]
    attn_got[1, 0] = attn_send[1, y * 2 + c]
    for across, place_to, r in ((0, 2, 2), (1, 2, 4), (0, 3, 3), (1, 3, 5), (0, 1, 1), (1, 1, 1)):
        to, number = peer(r), across * 4 + place_to
        near = (to // 2) % 2 if across == 0 else to // 4
        attn[number] = remote(
            attn_send.at[across, near * 2 + to % 2],
            attn_got.at[across, place_to],
            attn_ss.at[number],
            attn_rs.at[number],
            (z, to),
        )
    for r in range(1, experts):
        dots[r] = remote(
            dots_send.at[peer(r)], dots_got.at[r], dots_ss.at[r], dots_rs.at[r], (z, peer(r))
        )


    def pass_on(k):
        along[layers - k].wait_recv()
        block = window.at[(z + k) % layers, window_rows(c)]
        swap[k] = remote(block, block, wt_ss.at[k], wt_rs.at[k], twin)

    pass_on(1)
    slots = lax.broadcasted_iota(jnp.int32, (SLOTS, tokens), 0)

    def row_of(values, expert):
        return jnp.sum(jnp.where(names == expert, values, 0.0), axis=0, keepdims=True)

    shares = {}

    def make_share(q):
        if q:
            info[q].wait_recv()
            place_q, gate_q = info_got[q, 0], info_got[q, 1]
        else:
            place_q, gate_q = place, gate
        share = jnp.concatenate(
            [
                jnp.where(
                    slots == row_of(place_q, expert).astype(jnp.int32),
                    row_of(gate_q, expert),
                    0.0,
                )
                for expert in (e, peer(1))
            ],
            axis=0,
        )
        shares[q] = split_columns(share)
        rows[q].wait_recv()

    start = (chip * 2 * shard) // 128 * 128
    width = window.shape[1]

    def slab_of(k):
        return columns(((z + k) % layers) * slab, slab)

    def add_rows(q, k):
        here = slab_of(k)
        both = lax.dot_general(
            shares[q], blocks[q, :, here], CONTRACT_FIRST, preferred_element_type=jnp.float32
        )
        part[q, :, here] = both[:tokens] + both[tokens:]

    def add_key(q, k):
        here = columns(((z + k) % layers) * slab + start, width)
        part[q, :, here] += lax.dot_general(
            cots[2 * q],
            window[(z + k) % layers],
            CONTRACT_LAST,
            preferred_element_type=jnp.float32,
        )

    to_x, to_y = (z, peer(2)), (z, peer(4))
    x_first = [(to_x, x_got), (to_y, y_got)]
    relays, direct, onward = {}, {}, {}

    def send_slab(q, k, dst, number, to):
        here = slab_of(k)
        return remote(
            send.at[q, :, here], dst.at[:, here], part_ss.at[number], part_rs.at[number], to
        )

    make_share(3)
    for k in range(layers):
        add_rows(3, k)
    cot[3].wait_recv()
    cot[4].wait_recv()
    for k in range(layers):
        swap[k].wait_recv()
        add_key(3, k)
        here = slab_of(k)
        send[3, :, here] = part[3, :, here].astype(jnp.bfloat16)
        relays[k] = send_slab(3, k, relay_got, k, x_first[k % 2][0])
        if k == 1:
            pick_rows((1, 2))
            pass_on(2)
            pass_on(3)

    for copy in [*forward.values(), *attn.values()]:
        copy.wait_recv()
    for across in range(2):
        near_cots = jnp.concatenate([cots[0:2], cots[2 + 2 * across : 4 + 2 * across]], axis=0)
        grad = lax.dot_general(
            attn_got[across].reshape(4 * tokens, layers * shard),
            near_cots.reshape(4 * tokens, keys),
            CONTRACT_FIRST,
            preferred_element_type=jnp.float32,
        ).reshape(layers, shard, keys)
        grad_own[:, across * shard : (across + 1) * shard, :] = grad
        grad_send[:, across * shard : (across + 1) * shard, :] = grad.astype(jnp.bfloat16)
    outward = {}
    for rz in (2, 1, 3):
        to = (z + rz) % layers
        outward[rz] = remote(
            grad_send.at[to], grad_got.at[rz], gz_ss.at[rz], gz_rs.at[rz], (to, e)
        )
    make_share(1)
    make_share(2)
    for k in range(layers):
        q, (to, dst) = k % 2 + 1, x_first[k % 2]
        add_rows(q, k)
        add_key(q, k)
        here = slab_of(k)
        send[q, :, here] = part[q, :, here].astype(jnp.bfloat16)
        direct[k] = send_slab(q, k, dst, layers + k, to)
    for k in range(layers):
        q, (to, dst) = 2 - k % 2, x_first[1 - k % 2]
        add_rows(q, k)
        add_key(q, k)
        relays[k].wait_recv()
        here = slab_of(k)
        send[q, :, here] = (
            part[q, :, here] + relay_got[:, here].astype(jnp.float32)
        ).astype(jnp.bfloat16)
        onward[k] = send_slab(q, k, dst, 2 * layers + k, to)

    pick_rows((0,))
    inner = jnp.zeros((experts, tokens), jnp.float32)
    for r in range(experts):
        if r > 0:
            dots[r].wait_recv()
            got = dots_got[r, :, 0:SLOTS]
        else:
            got = dots_send[e, :, 0:SLOTS]
        expert = peer(r)
        hit = (slots == row_of(place, expert).astype(jnp.int32)).astype(jnp.float32)
        found = jnp.dot(
            got.astype(jnp.bfloat16),
            hit.astype(jnp.bfloat16),
            preferred_element_type=jnp.float32,
        )
        inner = inner + jnp.where(names == expert, found[0:1, :], 0.0)
    mean_inner = jnp.sum(gate * inner, axis=0, keepdims=True)
    d_probs = choose * (inner - mean_inner) / chosen_sum
    d_logits = probs * (d_probs - jnp.sum(probs * d_probs, axis=0, keepdims=True))
    d_parts = split_columns(d_logits)

    make_share(0)
    for k in range(layers):
        add_rows(0, k)
        add_key(0, k)

    loads[7].wait()

    def router_tile(i, _):
        here = columns(i * slab, slab)
        both = lax.dot_general(
            d_parts, router_ref[:, here], CONTRACT_FIRST, preferred_element_type=jnp.float32
        )
        part[0, :, here] += both[:tokens] + both[tokens:]
        return 0

    lax.fori_loop(0, layers, router_tile, 0)

    for rz in range(1, layers):
        outward[rz].wait_recv()
    grad_own[0] = (
        grad_own[z]
        + grad_got[1].astype(jnp.float32)
        + grad_got[2].astype(jnp.float32)
        + grad_got[3].astype(jnp.float32)
    )
    final = {}
    for across, mine_o, r in ((0, y, 4), (1, x, 2)):
        other = pl.ds(pl.multiple_of(across * shard + (1 - mine_o) * bit, 16), bit)
        cross_send[across] = grad_own[0, other, :].astype(jnp.bfloat16)
        final[across] = remote(
            cross_send.at[across],
            cross_got.at[across],
            gx_ss.at[across],
            gx_rs.at[across],
            (z, peer(r)),
        )
    for k in range(layers):
        direct[k].wait_recv()
        onward[k].wait_recv()
        here = slab_of(k)
        out_ref[:, here] = (
            part[0, :, here]
            + x_got[:, here].astype(jnp.float32)
            + y_got[:, here].astype(jnp.float32)
        ).astype(jnp.bfloat16)
    for across, mine_o in ((0, y), (1, x)):
        final[across].wait_recv()
        kept = pl.ds(pl.multiple_of(across * shard + mine_o * bit, 16), bit)
        grad_ref[across * bit : (across + 1) * bit, :] = grad_own[0, kept, :] + cross_got[
            across
        ].astype(jnp.float32)
    for group in (info, cot, attn, dots, rows, forward, outward, final):
        for copy in group.values():
            copy.wait_send()
    for group in (along, swap, relays, direct, onward):
        for copy in group.values():
            copy.wait_send()


def fused_local(
    attn_input,
    key_cot,
    routing,
    router_base,
    router_weight,
    expert_rows,
    expert_dots,
    key_weight,
    first_moment,
    second_moment,
):
    tokens, features = attn_input.shape
    experts, capacity, _ = expert_rows.shape
    shard, keys = key_weight.shape
    layers = lax.axis_size("dp")
    b16, f32 = jnp.bfloat16, jnp.float32
    vmem, anywhere = pl.BlockSpec(memory_space=pltpu.VMEM), pl.BlockSpec(memory_space=pl.ANY)
    dma = pltpu.SemaphoreType.DMA
    input_grad, key_grad = pl.pallas_call(
        fused,
        out_shape=(
            pltpu.VMEM((tokens, features), b16),
            pltpu.VMEM((shard, keys), f32),
        ),
        in_specs=[anywhere] * 8,
        out_specs=[vmem] * 2,
        scratch_shapes=[
            pltpu.VMEM((tokens, features), b16),
            pltpu.VMEM(routing.shape[::-1], jnp.int32),
            pltpu.VMEM(router_base.shape[::-1], f32),
            pltpu.VMEM(router_weight.shape[::-1], b16),
            pltpu.VMEM(expert_dots.shape, b16),
            pltpu.VMEM((shard, keys), f32),
            pltpu.VMEM((experts * capacity, features), b16),
            pltpu.VMEM((4, SLOTS, features), b16),
            pltpu.VMEM((4, 2 * SLOTS, features), b16),
            pltpu.VMEM((2, experts, tokens), f32),
            pltpu.VMEM((4, 2, experts, tokens), f32),
            pltpu.VMEM((experts, 8, 128), f32),
            pltpu.VMEM((experts, 8, 128), f32),
            pltpu.VMEM((experts, tokens, keys), b16),
            pltpu.VMEM((2, 4, tokens, layers * shard), b16),
            pltpu.VMEM((2, 4, tokens, layers * shard), b16),
            pltpu.VMEM((layers, 2 * shard + 64, keys), b16),
            pltpu.VMEM((4, tokens, features), f32),
            pltpu.VMEM((4, tokens, features), b16),
            pltpu.VMEM((tokens, features), b16),
            pltpu.VMEM((tokens, features), b16),
            pltpu.VMEM((tokens, features), b16),
            pltpu.VMEM((layers, 2 * shard, keys), f32),
            pltpu.VMEM((layers, 2 * shard, keys), b16),
            pltpu.VMEM((layers, 2 * shard, keys), b16),
            pltpu.VMEM((2, shard // 2, keys), b16),
            pltpu.VMEM((2, shard // 2, keys), b16),
            dma((8,)),
            dma((4,)),
            dma((4,)),
            dma((4,)),
            dma((4,)),
            dma((experts,)),
            dma((experts,)),
            dma((5,)),
            dma((5,)),
            dma((4,)),
            dma((4,)),
            dma((experts,)),
            dma((experts,)),
            dma((layers,)),
            dma((layers,)),
            dma((layers,)),
            dma((layers,)),
            dma((3 * layers,)),
            dma((3 * layers,)),
            dma((layers,)),
            dma((layers,)),
            dma((2,)),
            dma((2,)),
        ],
        compiler_params=pltpu.CompilerParams(
            collective_id=0, has_side_effects=True, vmem_limit_bytes=60 * 1024 * 1024
        ),
        cost_estimate=pl.CostEstimate(
            flops=6 * 10**9, bytes_accessed=10**7, transcendentals=10**4
        ),
    )(
        attn_input,
        key_cot,
        routing.T,
        router_base.T,
        router_weight.T,
        expert_rows.transpose(1, 0, 2).reshape(capacity * experts, features),
        expert_dots,
        key_weight,
    )
    return (input_grad, *adamw(key_weight, first_moment, second_moment, key_grad))


def solution(mesh):
    fits = mesh.shape["dp"] == 4 and mesh.shape["expert"] == 8
    in_specs = (
        P(("dp", "expert"), None),
        P(("dp", "expert"), None),
        P(("dp", "expert"), None),
        P(("dp", "expert"), None),
        P(),
        P(("dp", "expert"), None, None),
        P(("dp", "expert"), None),
        P(("dp", "expert"), None),
        P(("dp", "expert"), None),
        P(("dp", "expert"), None),
    )
    out_specs = (
        P(("dp", "expert"), None),
        P(("dp", "expert"), None),
        P(("dp", "expert"), None),
        P(("dp", "expert"), None),
    )
    return jax.shard_map(
        fused_local if fits else local, mesh=mesh, in_specs=in_specs, out_specs=out_specs, check_vma=False)
```

```python
import jax
import jax.numpy as jnp
from jax import lax
from jax.experimental import pallas as pl
from jax.experimental.pallas import tpu as pltpu
from jax.sharding import PartitionSpec as P

ADAM_STEP = 10


beta_one = 0.9
beta_two = 0.95
epsilon = 1e-08
learn_rate = 0.005
decay_rate = 0.1
routed_offset = 3.5


def route_slots(routing, experts, capacity):
    choose = (routing[:, :, None] == jnp.arange(experts, dtype=jnp.int32)[None, None, :]).astype(
        jnp.int32
    )
    per_expert = jnp.sum(choose, axis=1)
    before = jnp.cumsum(per_expert, axis=0) - per_expert
    slots = jnp.sum(choose * before[:, None, :], axis=2)
    return (choose, routing * capacity + slots)


def combine(routing, router_base, returned, returned_dots, router_weight):
    experts, capacity, features = returned.shape
    choose, flat_index = route_slots(routing, experts, capacity)
    routed_mask = jnp.sum(choose, axis=1).astype(jnp.float32)
    router_probs = jax.nn.softmax(router_base + routed_offset * routed_mask, axis=-1)
    picked = jnp.take(returned.reshape(experts * capacity, features), flat_index, axis=0)
    inner = jnp.take(returned_dots.reshape(experts * capacity), flat_index, axis=0).astype(
        jnp.float32
    )
    chosen = jnp.take_along_axis(router_probs, routing, axis=1)
    chosen_sum = jnp.sum(chosen, axis=1, keepdims=True)
    gate_share = chosen / chosen_sum
    mixed = gate_share[:, 0:1] * picked[:, 0].astype(jnp.float32)
    for position in range(1, routing.shape[1]):
        mixed = mixed + gate_share[:, position : position + 1] * picked[:, position].astype(
            jnp.float32
        )
    mean_inner = jnp.sum(gate_share * inner, axis=1, keepdims=True)
    d_chosen = (inner - mean_inner) / chosen_sum
    d_probs = jnp.sum(choose.astype(jnp.float32) * d_chosen[:, :, None], axis=1)
    d_logits = router_probs * (d_probs - jnp.sum(router_probs * d_probs, axis=1, keepdims=True))
    router_term = jnp.dot(
        d_logits, router_weight.astype(jnp.float32).T, precision=lax.Precision.HIGHEST
    )
    return mixed + router_term


def adamw(weight, first, second, grad):
    new_first = beta_one * first + (1.0 - beta_one) * grad
    new_second = beta_two * second + (1.0 - beta_two) * grad * grad
    first_hat = new_first / (1.0 - beta_one**ADAM_STEP)
    second_hat = new_second / (1.0 - beta_two**ADAM_STEP)
    new_weight = weight - learn_rate * (
        first_hat / (jnp.sqrt(second_hat) + epsilon) + decay_rate * weight
    )
    return (new_weight, new_first, new_second)


def local(
    attn_input,
    key_cot,
    routing,
    router_base,
    router_weight,
    expert_rows,
    expert_dots,
    key_weight,
    first_moment,
    second_moment,
):
    returned, returned_dots = (
        lax.all_to_all(expert_rows, "expert", split_axis=0, concat_axis=0, tiled=True),
        lax.all_to_all(expert_dots, "expert", split_axis=0, concat_axis=0, tiled=True),
    )
    moe_term = combine(routing, router_base, returned, returned_dots, router_weight)
    key_term = lax.dot_general(
        key_cot,
        lax.all_gather(key_weight.astype(jnp.bfloat16), ("dp", "expert"), axis=0, tiled=True),
        (((1,), (1,)), ((), ())),
        preferred_element_type=jnp.float32,
    )
    input_grad = (moe_term + key_term).astype(jnp.bfloat16)
    partial_grad = lax.dot_general(
        attn_input, key_cot, (((0,), (0,)), ((), ())), preferred_element_type=jnp.float32
    )
    cycle_size = lax.axis_size("dp")
    group_size = lax.axis_size("expert")
    shard_rows = key_weight.shape[0]
    stacked = partial_grad.reshape(cycle_size, group_size * shard_rows, partial_grad.shape[1])
    halfway = lax.psum_scatter(stacked.astype(jnp.bfloat16), "dp", scatter_dimension=0, tiled=True)
    summed = lax.psum_scatter(halfway, "expert", scatter_dimension=1, tiled=True).astype(
        jnp.float32
    )
    key_grad = summed.reshape(shard_rows, partial_grad.shape[1])
    new_key_weight, new_first_moment, new_second_moment = adamw(
        key_weight, first_moment, second_moment, key_grad
    )
    return (input_grad, new_key_weight, new_first_moment, new_second_moment)


MESH = pl.DeviceIdType.MESH
CONTRACT_FIRST = (((0,), (0,)), ((), ()))
CONTRACT_LAST = (((1,), (1,)), ((), ()))
SLOTS = 80


def split_columns(values):
    high = values.astype(jnp.bfloat16)
    low = (values - high.astype(jnp.float32)).astype(jnp.bfloat16)
    return jnp.concatenate([high, low], axis=1)


def fused(
    attn_hbm,
    cot_hbm,
    routing_hbm,
    base_hbm,
    router_hbm,
    rows_hbm,
    dots_hbm,
    weight_hbm,
    out_ref,
    grad_ref,
    attn_ref,
    routing_ref,
    base_ref,
    router_ref,
    dots_ref,
    weight_ref,
    rows_own,
    picked,
    blocks,
    info_send,
    info_got,
    dots_send,
    dots_got,
    cots,
    attn_send,
    attn_got,
    window,
    part,
    send,
    relay_got,
    x_got,
    y_got,
    grad_own,
    grad_send,
    grad_got,
    cross_send,
    cross_got,
    local_sem,
    info_ss,
    info_rs,
    rows_ss,
    rows_rs,
    dots_ss,
    dots_rs,
    cot_ss,
    cot_rs,
    twin_ss,
    twin_rs,
    attn_ss,
    attn_rs,
    wz_ss,
    wz_rs,
    wt_ss,
    wt_rs,
    part_ss,
    part_rs,
    gz_ss,
    gz_rs,
    gx_ss,
    gx_rs,
):
    tokens, features = out_ref.shape
    experts, capacity = dots_ref.shape
    shard, keys = weight_ref.shape
    layers = window.shape[0]
    slab = features // layers
    z, e = lax.axis_index("dp"), lax.axis_index("expert")
    y, x, c = e // 4, (e // 2) % 2, e % 2
    chip = e // 2

    def peer(r):
        return ((y + r // 4) % 2) * 4 + ((x + (r // 2) % 2) % 2) * 2 + (c + r % 2) % 2

    def columns(start, size):
        return pl.ds(pl.multiple_of(start, 128), size)

    def remote(src, dst, send_sem, recv_sem, to):
        copy = pltpu.make_async_remote_copy(
            src_ref=src,
            dst_ref=dst,
            send_sem=send_sem,
            recv_sem=recv_sem,
            device_id=to,
            device_id_type=MESH,
        )
        copy.start()
        return copy

    barrier = pltpu.get_barrier_semaphore()
    for r in range(1, experts):
        pl.semaphore_signal(barrier, inc=1, device_id=(z, peer(r)), device_id_type=MESH)
    for rz in range(1, layers):
        pl.semaphore_signal(
            barrier, inc=1, device_id=((z + rz) % layers, e), device_id_type=MESH
        )
    loads = [
        pltpu.make_async_copy(src, dst, local_sem.at[i])
        for i, (src, dst) in enumerate(
            (
                (routing_hbm, routing_ref),
                (base_hbm, base_ref),
                (weight_hbm, weight_ref),
                (dots_hbm, dots_ref),
                (cot_hbm, cots.at[0]),
                (attn_hbm, attn_ref),
                (rows_hbm, rows_own),
                (router_hbm, router_ref),
            )
        )
    ]
    for load in loads:
        load.start()

    shift = 64 * (chip % 2)

    def window_rows(core):
        return pl.ds(pl.multiple_of(shift + core * shard, 32), shard)

    loads[2].wait()
    window[z, window_rows(c), :] = weight_ref[...].astype(jnp.bfloat16)
    spare = pl.ds(pl.multiple_of(2 * shard * (1 - chip % 2), 64), 64)
    for i in range(layers):
        window[i, spare, :] = jnp.zeros((64, keys), jnp.bfloat16)

    loads[4].wait()
    pl.semaphore_wait(barrier, experts - 1 + layers - 1)

    twin = (z, peer(1))
    info, cot, attn, dots, rows = {}, {}, {}, {}, {}
    mine = window.at[z, window_rows(c)]
    swap = {0: remote(mine, mine, wt_ss.at[0], wt_rs.at[0], twin)}
    along = {
        rz: remote(mine, mine, wz_ss.at[rz], wz_rs.at[rz], ((z + rz) % layers, e))
        for rz in (3, 2, 1)
    }
    for q in (1, 2):
        cot[q] = remote(
            cots.at[0], cots.at[2 * q], cot_ss.at[q], cot_rs.at[q], (z, peer(2 * q))
        )
    forward = {0: remote(cots.at[0], cots.at[1], twin_ss.at[0], twin_rs.at[0], twin)}
    for i in (0, 1, 3):
        loads[i].wait()
    routing = routing_ref[...]
    names = lax.broadcasted_iota(jnp.int32, (experts, tokens), 0)
    choose = jnp.zeros((experts, tokens), jnp.float32)
    for k in range(routing.shape[0]):
        choose = choose + (routing[k : k + 1, :] == names).astype(jnp.float32)
    earlier = (
        lax.broadcasted_iota(jnp.int32, (tokens, tokens), 0)
        < lax.broadcasted_iota(jnp.int32, (tokens, tokens), 1)
    ).astype(jnp.bfloat16)
    before = jnp.dot(choose.astype(jnp.bfloat16), earlier, preferred_element_type=jnp.float32)
    place = jnp.where(choose > 0.0, before, -1.0)
    logits = base_ref[...] + routed_offset * choose
    raised = jnp.exp(logits - jnp.max(logits, axis=0, keepdims=True))
    probs = raised / jnp.sum(raised, axis=0, keepdims=True)
    chosen = probs * choose
    chosen_sum = jnp.sum(chosen, axis=0, keepdims=True)
    gate = chosen / chosen_sum
    info_send[0] = place
    info_send[1] = gate

    dots_all = dots_ref[...].astype(jnp.float32)
    dots_send[...] = jnp.zeros_like(dots_send)
    for j in range(experts):
        dots_send[j, :, 0:capacity] = jnp.broadcast_to(dots_all[j : j + 1, :], (8, capacity))
    for q in (3, 1, 2):
        info[q] = remote(
            info_send, info_got.at[q], info_ss.at[q], info_rs.at[q], (z, peer(2 * q))
        )
    loads[6].wait()
    cell = lax.broadcasted_iota(jnp.int32, (SLOTS, experts * capacity), 1)
    first_cell = experts * lax.broadcasted_iota(jnp.int32, (SLOTS, experts * capacity), 0)

    def pick_rows(group):
        pick = jnp.concatenate(
            [
                (cell == first_cell + peer(r)).astype(jnp.float32).astype(jnp.bfloat16)
                for q in group
                for r in (2 * q + 1, 2 * q)
            ],
            axis=0,
        )

        def tile(i, _):
            here = columns(i * slab, slab)
            got = jnp.dot(pick, rows_own[:, here], preferred_element_type=jnp.float32)
            got = got.astype(jnp.bfloat16)
            for k, q in enumerate(group):
                picked[q, :, here] = got[2 * k * SLOTS : (2 * k + 1) * SLOTS]
                blocks[q, 0:SLOTS, here] = got[(2 * k + 1) * SLOTS : (2 * k + 2) * SLOTS]
            return 0

        lax.fori_loop(0, layers, tile, 0)
        for q in group:
            rows[q] = remote(
                picked.at[q],
                blocks.at[q, pl.ds(SLOTS, SLOTS)],
                rows_ss.at[q],
                rows_rs.at[q],
                twin,
            )

    pick_rows((3,))
    for q in (1, 2):
        cot[q].wait_recv()
        piece = pl.ds((q - 1) * (tokens // 2), tokens // 2)
        cot[2 + q] = remote(
            cots.at[2 * q, piece],
            cots.at[6, piece],
            cot_ss.at[2 + q],
            cot_rs.at[2 + q],
            (z, peer(6 - 2 * q)),
        )
        forward[q] = remote(
            cots.at[2 * q], cots.at[2 * q + 1], twin_ss.at[q], twin_rs.at[q], twin
        )
    loads[5].wait()
    bit = shard // 2
    for across in range(2):
        for near in range(2):
            for core in range(2):
                starts = [
                    i * slab
                    + (near * (4, 2)[1 - across] + far * (4, 2)[across] + core) * shard
                    + across * bit
                    for i in range(layers)
                    for far in range(2)
                ]
                attn_send[across, near * 2 + core] = jnp.concatenate(
                    [attn_ref[:, start : start + bit] for start in starts], axis=1
                )
    attn_got[0, 0] = attn_send[0, x * 2 + c]
    attn_got[1, 0] = attn_send[1, y * 2 + c]
    for across, place_to, r in ((0, 2, 2), (1, 2, 4), (0, 3, 3), (1, 3, 5), (0, 1, 1), (1, 1, 1)):
        to, number = peer(r), across * 4 + place_to
        near = (to // 2) % 2 if across == 0 else to // 4
        attn[number] = remote(
            attn_send.at[across, near * 2 + to % 2],
            attn_got.at[across, place_to],
            attn_ss.at[number],
            attn_rs.at[number],
            (z, to),
        )
    for r in range(1, experts):
        dots[r] = remote(
            dots_send.at[peer(r)], dots_got.at[r], dots_ss.at[r], dots_rs.at[r], (z, peer(r))
        )


    def pass_on(k):
        along[layers - k].wait_recv()
        block = window.at[(z + k) % layers, window_rows(c)]
        swap[k] = remote(block, block, wt_ss.at[k], wt_rs.at[k], twin)

    pass_on(1)
    slots = lax.broadcasted_iota(jnp.int32, (SLOTS, tokens), 0)

    def row_of(values, expert):
        return jnp.sum(jnp.where(names == expert, values, 0.0), axis=0, keepdims=True)

    shares = {}

    def make_share(q):
        if q:
            info[q].wait_recv()
            place_q, gate_q = info_got[q, 0], info_got[q, 1]
        else:
            place_q, gate_q = place, gate
        share = jnp.concatenate(
            [
                jnp.where(
                    slots == row_of(place_q, expert).astype(jnp.int32),
                    row_of(gate_q, expert),
                    0.0,
                )
                for expert in (e, peer(1))
            ],
            axis=0,
        )
        shares[q] = share.astype(jnp.bfloat16)
        rows[q].wait_recv()

    start = (chip * 2 * shard) // 128 * 128
    width = window.shape[1]

    def slab_of(k):
        return columns(((z + k) % layers) * slab, slab)

    def add_rows(q, k):
        here = slab_of(k)
        part[q, :, here] = lax.dot_general(
            shares[q], blocks[q, :, here], CONTRACT_FIRST, preferred_element_type=jnp.float32
        )

    def add_key(q, k):
        here = columns(((z + k) % layers) * slab + start, width)
        part[q, :, here] += lax.dot_general(
            cots[2 * q],
            window[(z + k) % layers],
            CONTRACT_LAST,
            preferred_element_type=jnp.float32,
        )

    to_x, to_y = (z, peer(2)), (z, peer(4))
    x_first = [(to_x, x_got), (to_y, y_got)]
    relays, direct, onward = {}, {}, {}

    def send_slab(q, k, dst, number, to):
        here = slab_of(k)
        return remote(
            send.at[q, :, here], dst.at[:, here], part_ss.at[number], part_rs.at[number], to
        )

    make_share(3)
    for k in range(layers):
        add_rows(3, k)
    cot[3].wait_recv()
    cot[4].wait_recv()
    for k in range(layers):
        swap[k].wait_recv()
        add_key(3, k)
        here = slab_of(k)
        send[3, :, here] = part[3, :, here].astype(jnp.bfloat16)
        relays[k] = send_slab(3, k, relay_got, k, x_first[k % 2][0])
        if k == 1:
            pass_on(2)
            pass_on(3)

    for copy in [*forward.values(), *attn.values()]:
        copy.wait_recv()
    for across in range(2):
        near_cots = jnp.concatenate([cots[0:2], cots[2 + 2 * across : 4 + 2 * across]], axis=0)
        grad = lax.dot_general(
            attn_got[across].reshape(4 * tokens, layers * shard),
            near_cots.reshape(4 * tokens, keys),
            CONTRACT_FIRST,
            preferred_element_type=jnp.float32,
        ).reshape(layers, shard, keys)
        grad_own[:, across * shard : (across + 1) * shard, :] = grad
        grad_send[:, across * shard : (across + 1) * shard, :] = grad.astype(jnp.bfloat16)
    outward = {}
    for rz in (2, 1, 3):
        to = (z + rz) % layers
        outward[rz] = remote(
            grad_send.at[to], grad_got.at[rz], gz_ss.at[rz], gz_rs.at[rz], (to, e)
        )
    pick_rows((1, 2))
    make_share(1)
    make_share(2)
    for k in range(layers):
        q, (to, dst) = k % 2 + 1, x_first[k % 2]
        add_rows(q, k)
        add_key(q, k)
        here = slab_of(k)
        send[q, :, here] = part[q, :, here].astype(jnp.bfloat16)
        direct[k] = send_slab(q, k, dst, layers + k, to)
    for k in range(layers):
        q, (to, dst) = 2 - k % 2, x_first[1 - k % 2]
        add_rows(q, k)
        add_key(q, k)
        relays[k].wait_recv()
        here = slab_of(k)
        send[q, :, here] = (
            part[q, :, here] + relay_got[:, here].astype(jnp.float32)
        ).astype(jnp.bfloat16)
        onward[k] = send_slab(q, k, dst, 2 * layers + k, to)

    pick_rows((0,))
    inner = jnp.zeros((experts, tokens), jnp.float32)
    for r in range(experts):
        if r > 0:
            dots[r].wait_recv()
            got = dots_got[r, :, 0:SLOTS]
        else:
            got = dots_send[e, :, 0:SLOTS]
        expert = peer(r)
        hit = (slots == row_of(place, expert).astype(jnp.int32)).astype(jnp.float32)
        found = jnp.dot(
            got.astype(jnp.bfloat16),
            hit.astype(jnp.bfloat16),
            preferred_element_type=jnp.float32,
        )
        inner = inner + jnp.where(names == expert, found[0:1, :], 0.0)
    mean_inner = jnp.sum(gate * inner, axis=0, keepdims=True)
    d_probs = choose * (inner - mean_inner) / chosen_sum
    d_logits = probs * (d_probs - jnp.sum(probs * d_probs, axis=0, keepdims=True))
    d_parts = split_columns(d_logits)

    make_share(0)
    for k in range(layers):
        add_rows(0, k)
        add_key(0, k)

    loads[7].wait()

    def router_tile(i, _):
        here = columns(i * slab, slab)
        both = lax.dot_general(
            d_parts, router_ref[:, here], CONTRACT_FIRST, preferred_element_type=jnp.float32
        )
        part[0, :, here] += both[:tokens] + both[tokens:]
        return 0

    lax.fori_loop(0, layers, router_tile, 0)

    for rz in range(1, layers):
        outward[rz].wait_recv()
    grad_own[0] = (
        grad_own[z]
        + grad_got[1].astype(jnp.float32)
        + grad_got[2].astype(jnp.float32)
        + grad_got[3].astype(jnp.float32)
    )
    final = {}
    for across, mine_o, r in ((0, y, 4), (1, x, 2)):
        other = pl.ds(pl.multiple_of(across * shard + (1 - mine_o) * bit, 16), bit)
        cross_send[across] = grad_own[0, other, :].astype(jnp.bfloat16)
        final[across] = remote(
            cross_send.at[across],
            cross_got.at[across],
            gx_ss.at[across],
            gx_rs.at[across],
            (z, peer(r)),
        )
    for k in range(layers):
        direct[k].wait_recv()
        onward[k].wait_recv()
        here = slab_of(k)
        out_ref[:, here] = (
            part[0, :, here]
            + x_got[:, here].astype(jnp.float32)
            + y_got[:, here].astype(jnp.float32)
        ).astype(jnp.bfloat16)
    for across, mine_o in ((0, y), (1, x)):
        final[across].wait_recv()
        kept = pl.ds(pl.multiple_of(across * shard + mine_o * bit, 16), bit)
        grad_ref[across * bit : (across + 1) * bit, :] = grad_own[0, kept, :] + cross_got[
            across
        ].astype(jnp.float32)
    for group in (info, cot, attn, dots, rows, forward, outward, final):
        for copy in group.values():
            copy.wait_send()
    for group in (along, swap, relays, direct, onward):
        for copy in group.values():
            copy.wait_send()


def fused_local(
    attn_input,
    key_cot,
    routing,
    router_base,
    router_weight,
    expert_rows,
    expert_dots,
    key_weight,
    first_moment,
    second_moment,
):
    tokens, features = attn_input.shape
    experts, capacity, _ = expert_rows.shape
    shard, keys = key_weight.shape
    layers = lax.axis_size("dp")
    b16, f32 = jnp.bfloat16, jnp.float32
    vmem, anywhere = pl.BlockSpec(memory_space=pltpu.VMEM), pl.BlockSpec(memory_space=pl.ANY)
    dma = pltpu.SemaphoreType.DMA
    input_grad, key_grad = pl.pallas_call(
        fused,
        out_shape=(
            pltpu.VMEM((tokens, features), b16),
            pltpu.VMEM((shard, keys), f32),
        ),
        in_specs=[anywhere] * 8,
        out_specs=[vmem] * 2,
        scratch_shapes=[
            pltpu.VMEM((tokens, features), b16),
            pltpu.VMEM(routing.shape[::-1], jnp.int32),
            pltpu.VMEM(router_base.shape[::-1], f32),
            pltpu.VMEM(router_weight.shape[::-1], b16),
            pltpu.VMEM(expert_dots.shape, b16),
            pltpu.VMEM((shard, keys), f32),
            pltpu.VMEM((experts * capacity, features), b16),
            pltpu.VMEM((4, SLOTS, features), b16),
            pltpu.VMEM((4, 2 * SLOTS, features), b16),
            pltpu.VMEM((2, experts, tokens), f32),
            pltpu.VMEM((4, 2, experts, tokens), f32),
            pltpu.VMEM((experts, 8, 128), f32),
            pltpu.VMEM((experts, 8, 128), f32),
            pltpu.VMEM((experts, tokens, keys), b16),
            pltpu.VMEM((2, 4, tokens, layers * shard), b16),
            pltpu.VMEM((2, 4, tokens, layers * shard), b16),
            pltpu.VMEM((layers, 2 * shard + 64, keys), b16),
            pltpu.VMEM((4, tokens, features), f32),
            pltpu.VMEM((4, tokens, features), b16),
            pltpu.VMEM((tokens, features), b16),
            pltpu.VMEM((tokens, features), b16),
            pltpu.VMEM((tokens, features), b16),
            pltpu.VMEM((layers, 2 * shard, keys), f32),
            pltpu.VMEM((layers, 2 * shard, keys), b16),
            pltpu.VMEM((layers, 2 * shard, keys), b16),
            pltpu.VMEM((2, shard // 2, keys), b16),
            pltpu.VMEM((2, shard // 2, keys), b16),
            dma((8,)),
            dma((4,)),
            dma((4,)),
            dma((4,)),
            dma((4,)),
            dma((experts,)),
            dma((experts,)),
            dma((5,)),
            dma((5,)),
            dma((4,)),
            dma((4,)),
            dma((experts,)),
            dma((experts,)),
            dma((layers,)),
            dma((layers,)),
            dma((layers,)),
            dma((layers,)),
            dma((3 * layers,)),
            dma((3 * layers,)),
            dma((layers,)),
            dma((layers,)),
            dma((2,)),
            dma((2,)),
        ],
        compiler_params=pltpu.CompilerParams(
            collective_id=0, has_side_effects=True, vmem_limit_bytes=60 * 1024 * 1024
        ),
        cost_estimate=pl.CostEstimate(
            flops=6 * 10**9, bytes_accessed=10**7, transcendentals=10**4
        ),
    )(
        attn_input,
        key_cot,
        routing.T,
        router_base.T,
        router_weight.T,
        expert_rows.transpose(1, 0, 2).reshape(capacity * experts, features),
        expert_dots,
        key_weight,
    )
    return (input_grad, *adamw(key_weight, first_moment, second_moment, key_grad))


def solution(mesh):
    fits = mesh.shape["dp"] == 4 and mesh.shape["expert"] == 8
    in_specs = (
        P(("dp", "expert"), None),
        P(("dp", "expert"), None),
        P(("dp", "expert"), None),
        P(("dp", "expert"), None),
        P(),
        P(("dp", "expert"), None, None),
        P(("dp", "expert"), None),
        P(("dp", "expert"), None),
        P(("dp", "expert"), None),
        P(("dp", "expert"), None),
    )
    out_specs = (
        P(("dp", "expert"), None),
        P(("dp", "expert"), None),
        P(("dp", "expert"), None),
        P(("dp", "expert"), None),
    )
    return jax.shard_map(
        fused_local if fits else local, mesh=mesh, in_specs=in_specs, out_specs=out_specs, check_vma=False)
```

```python
import jax
import jax.numpy as jnp
from jax import lax
from jax.experimental import pallas as pl
from jax.experimental.pallas import tpu as pltpu
from jax.sharding import PartitionSpec as P

ADAM_STEP = 10


beta_one = 0.9
beta_two = 0.95
epsilon = 1e-08
learn_rate = 0.005
decay_rate = 0.1
routed_offset = 3.5


def route_slots(routing, experts, capacity):
    choose = (routing[:, :, None] == jnp.arange(experts, dtype=jnp.int32)[None, None, :]).astype(
        jnp.int32
    )
    per_expert = jnp.sum(choose, axis=1)
    before = jnp.cumsum(per_expert, axis=0) - per_expert
    slots = jnp.sum(choose * before[:, None, :], axis=2)
    return (choose, routing * capacity + slots)


def combine(routing, router_base, returned, returned_dots, router_weight):
    experts, capacity, features = returned.shape
    choose, flat_index = route_slots(routing, experts, capacity)
    routed_mask = jnp.sum(choose, axis=1).astype(jnp.float32)
    router_probs = jax.nn.softmax(router_base + routed_offset * routed_mask, axis=-1)
    picked = jnp.take(returned.reshape(experts * capacity, features), flat_index, axis=0)
    inner = jnp.take(returned_dots.reshape(experts * capacity), flat_index, axis=0).astype(
        jnp.float32
    )
    chosen = jnp.take_along_axis(router_probs, routing, axis=1)
    chosen_sum = jnp.sum(chosen, axis=1, keepdims=True)
    gate_share = chosen / chosen_sum
    mixed = gate_share[:, 0:1] * picked[:, 0].astype(jnp.float32)
    for position in range(1, routing.shape[1]):
        mixed = mixed + gate_share[:, position : position + 1] * picked[:, position].astype(
            jnp.float32
        )
    mean_inner = jnp.sum(gate_share * inner, axis=1, keepdims=True)
    d_chosen = (inner - mean_inner) / chosen_sum
    d_probs = jnp.sum(choose.astype(jnp.float32) * d_chosen[:, :, None], axis=1)
    d_logits = router_probs * (d_probs - jnp.sum(router_probs * d_probs, axis=1, keepdims=True))
    router_term = jnp.dot(
        d_logits, router_weight.astype(jnp.float32).T, precision=lax.Precision.HIGHEST
    )
    return mixed + router_term


def adamw(weight, first, second, grad):
    new_first = beta_one * first + (1.0 - beta_one) * grad
    new_second = beta_two * second + (1.0 - beta_two) * grad * grad
    first_hat = new_first / (1.0 - beta_one**ADAM_STEP)
    second_hat = new_second / (1.0 - beta_two**ADAM_STEP)
    new_weight = weight - learn_rate * (
        first_hat / (jnp.sqrt(second_hat) + epsilon) + decay_rate * weight
    )
    return (new_weight, new_first, new_second)


def local(
    attn_input,
    key_cot,
    routing,
    router_base,
    router_weight,
    expert_rows,
    expert_dots,
    key_weight,
    first_moment,
    second_moment,
):
    returned, returned_dots = (
        lax.all_to_all(expert_rows, "expert", split_axis=0, concat_axis=0, tiled=True),
        lax.all_to_all(expert_dots, "expert", split_axis=0, concat_axis=0, tiled=True),
    )
    moe_term = combine(routing, router_base, returned, returned_dots, router_weight)
    key_term = lax.dot_general(
        key_cot,
        lax.all_gather(key_weight.astype(jnp.bfloat16), ("dp", "expert"), axis=0, tiled=True),
        (((1,), (1,)), ((), ())),
        preferred_element_type=jnp.float32,
    )
    input_grad = (moe_term + key_term).astype(jnp.bfloat16)
    partial_grad = lax.dot_general(
        attn_input, key_cot, (((0,), (0,)), ((), ())), preferred_element_type=jnp.float32
    )
    cycle_size = lax.axis_size("dp")
    group_size = lax.axis_size("expert")
    shard_rows = key_weight.shape[0]
    stacked = partial_grad.reshape(cycle_size, group_size * shard_rows, partial_grad.shape[1])
    halfway = lax.psum_scatter(stacked.astype(jnp.bfloat16), "dp", scatter_dimension=0, tiled=True)
    summed = lax.psum_scatter(halfway, "expert", scatter_dimension=1, tiled=True).astype(
        jnp.float32
    )
    key_grad = summed.reshape(shard_rows, partial_grad.shape[1])
    new_key_weight, new_first_moment, new_second_moment = adamw(
        key_weight, first_moment, second_moment, key_grad
    )
    return (input_grad, new_key_weight, new_first_moment, new_second_moment)


MESH = pl.DeviceIdType.MESH
CONTRACT_FIRST = (((0,), (0,)), ((), ()))
CONTRACT_LAST = (((1,), (1,)), ((), ()))
SLOTS = 80


def split_columns(values):
    high = values.astype(jnp.bfloat16)
    low = (values - high.astype(jnp.float32)).astype(jnp.bfloat16)
    return jnp.concatenate([high, low], axis=1)


def fused(
    attn_hbm,
    cot_hbm,
    routing_hbm,
    base_hbm,
    router_hbm,
    rows_hbm,
    dots_hbm,
    weight_hbm,
    out_ref,
    grad_ref,
    attn_ref,
    routing_ref,
    base_ref,
    router_ref,
    dots_ref,
    weight_ref,
    rows_own,
    picked,
    blocks,
    info_send,
    info_got,
    dots_send,
    dots_got,
    cots,
    attn_send,
    attn_got,
    window,
    part,
    send,
    relay_got,
    x_got,
    y_got,
    grad_own,
    grad_send,
    grad_got,
    cross_send,
    cross_got,
    local_sem,
    info_ss,
    info_rs,
    rows_ss,
    rows_rs,
    dots_ss,
    dots_rs,
    cot_ss,
    cot_rs,
    twin_ss,
    twin_rs,
    attn_ss,
    attn_rs,
    wz_ss,
    wz_rs,
    wt_ss,
    wt_rs,
    part_ss,
    part_rs,
    gz_ss,
    gz_rs,
    gx_ss,
    gx_rs,
):
    tokens, features = out_ref.shape
    experts, capacity = dots_ref.shape
    shard, keys = weight_ref.shape
    layers = window.shape[0]
    slab = features // layers
    z, e = lax.axis_index("dp"), lax.axis_index("expert")
    y, x, c = e // 4, (e // 2) % 2, e % 2
    chip = e // 2

    def peer(r):
        return ((y + r // 4) % 2) * 4 + ((x + (r // 2) % 2) % 2) * 2 + (c + r % 2) % 2

    def columns(start, size):
        return pl.ds(pl.multiple_of(start, 128), size)

    def remote(src, dst, send_sem, recv_sem, to):
        copy = pltpu.make_async_remote_copy(
            src_ref=src,
            dst_ref=dst,
            send_sem=send_sem,
            recv_sem=recv_sem,
            device_id=to,
            device_id_type=MESH,
        )
        copy.start()
        return copy

    barrier = pltpu.get_barrier_semaphore()
    for r in range(1, experts):
        pl.semaphore_signal(barrier, inc=1, device_id=(z, peer(r)), device_id_type=MESH)
    for rz in range(1, layers):
        pl.semaphore_signal(
            barrier, inc=1, device_id=((z + rz) % layers, e), device_id_type=MESH
        )
    loads = [
        pltpu.make_async_copy(src, dst, local_sem.at[i])
        for i, (src, dst) in enumerate(
            (
                (routing_hbm, routing_ref),
                (base_hbm, base_ref),
                (weight_hbm, weight_ref),
                (dots_hbm, dots_ref),
                (cot_hbm, cots.at[0]),
                (attn_hbm, attn_ref),
                (rows_hbm, rows_own),
                (router_hbm, router_ref),
            )
        )
    ]
    for load in loads:
        load.start()

    shift = 64 * (chip % 2)

    def window_rows(core):
        return pl.ds(pl.multiple_of(shift + core * shard, 32), shard)

    loads[2].wait()
    window[z, window_rows(c), :] = weight_ref[...].astype(jnp.bfloat16)
    spare = pl.ds(pl.multiple_of(2 * shard * (1 - chip % 2), 64), 64)
    for i in range(layers):
        window[i, spare, :] = jnp.zeros((64, keys), jnp.bfloat16)

    loads[4].wait()
    pl.semaphore_wait(barrier, experts - 1 + layers - 1)

    twin = (z, peer(1))
    info, cot, attn, dots, rows = {}, {}, {}, {}, {}
    mine = window.at[z, window_rows(c)]
    swap = {0: remote(mine, mine, wt_ss.at[0], wt_rs.at[0], twin)}
    along = {
        rz: remote(mine, mine, wz_ss.at[rz], wz_rs.at[rz], ((z + rz) % layers, e))
        for rz in (3, 2, 1)
    }
    for q in (1, 2):
        cot[q] = remote(
            cots.at[0], cots.at[2 * q], cot_ss.at[q], cot_rs.at[q], (z, peer(2 * q))
        )
    forward = {0: remote(cots.at[0], cots.at[1], twin_ss.at[0], twin_rs.at[0], twin)}
    for i in (0, 1, 3):
        loads[i].wait()
    routing = routing_ref[...]
    names = lax.broadcasted_iota(jnp.int32, (experts, tokens), 0)
    choose = jnp.zeros((experts, tokens), jnp.float32)
    for k in range(routing.shape[0]):
        choose = choose + (routing[k : k + 1, :] == names).astype(jnp.float32)
    earlier = (
        lax.broadcasted_iota(jnp.int32, (tokens, tokens), 0)
        < lax.broadcasted_iota(jnp.int32, (tokens, tokens), 1)
    ).astype(jnp.bfloat16)
    before = jnp.dot(choose.astype(jnp.bfloat16), earlier, preferred_element_type=jnp.float32)
    place = jnp.where(choose > 0.0, before, -1.0)
    logits = base_ref[...] + routed_offset * choose
    raised = jnp.exp(logits - jnp.max(logits, axis=0, keepdims=True))
    probs = raised / jnp.sum(raised, axis=0, keepdims=True)
    chosen = probs * choose
    chosen_sum = jnp.sum(chosen, axis=0, keepdims=True)
    gate = chosen / chosen_sum
    info_send[0] = place
    info_send[1] = gate

    dots_all = dots_ref[...].astype(jnp.float32)
    dots_send[...] = jnp.zeros_like(dots_send)
    for j in range(experts):
        dots_send[j, :, 0:capacity] = jnp.broadcast_to(dots_all[j : j + 1, :], (8, capacity))
    for q in (3, 1, 2):
        info[q] = remote(
            info_send, info_got.at[q], info_ss.at[q], info_rs.at[q], (z, peer(2 * q))
        )
    loads[6].wait()
    cell = lax.broadcasted_iota(jnp.int32, (SLOTS, experts * capacity), 1)
    first_cell = experts * lax.broadcasted_iota(jnp.int32, (SLOTS, experts * capacity), 0)

    def pick_rows(group):
        pick = jnp.concatenate(
            [
                (cell == first_cell + peer(r)).astype(jnp.float32).astype(jnp.bfloat16)
                for q in group
                for r in (2 * q + 1, 2 * q)
            ],
            axis=0,
        )

        def tile(i, _):
            here = columns(i * slab, slab)
            got = jnp.dot(pick, rows_own[:, here], preferred_element_type=jnp.float32)
            got = got.astype(jnp.bfloat16)
            for k, q in enumerate(group):
                picked[q, :, here] = got[2 * k * SLOTS : (2 * k + 1) * SLOTS]
                blocks[q, 0:SLOTS, here] = got[(2 * k + 1) * SLOTS : (2 * k + 2) * SLOTS]
            return 0

        lax.fori_loop(0, layers, tile, 0)
        for q in group:
            rows[q] = remote(
                picked.at[q],
                blocks.at[q, pl.ds(SLOTS, SLOTS)],
                rows_ss.at[q],
                rows_rs.at[q],
                twin,
            )

    loads[5].wait()
    bit = shard // 2
    for across in range(2):
        for near in range(2):
            for core in range(2):
                starts = [
                    i * slab
                    + (near * (4, 2)[1 - across] + far * (4, 2)[across] + core) * shard
                    + across * bit
                    for i in range(layers)
                    for far in range(2)
                ]
                attn_send[across, near * 2 + core] = jnp.concatenate(
                    [attn_ref[:, start : start + bit] for start in starts], axis=1
                )
    attn_got[0, 0] = attn_send[0, x * 2 + c]
    attn_got[1, 0] = attn_send[1, y * 2 + c]
    for across, place_to, r in ((0, 2, 2), (1, 2, 4), (0, 3, 3), (1, 3, 5), (0, 1, 1), (1, 1, 1)):
        to, number = peer(r), across * 4 + place_to
        near = (to // 2) % 2 if across == 0 else to // 4
        attn[number] = remote(
            attn_send.at[across, near * 2 + to % 2],
            attn_got.at[across, place_to],
            attn_ss.at[number],
            attn_rs.at[number],
            (z, to),
        )
    for r in range(1, experts):
        dots[r] = remote(
            dots_send.at[peer(r)], dots_got.at[r], dots_ss.at[r], dots_rs.at[r], (z, peer(r))
        )
    for q in (1, 2):
        cot[q].wait_recv()
        piece = pl.ds((q - 1) * (tokens // 2), tokens // 2)
        cot[2 + q] = remote(
            cots.at[2 * q, piece],
            cots.at[6, piece],
            cot_ss.at[2 + q],
            cot_rs.at[2 + q],
            (z, peer(6 - 2 * q)),
        )
        forward[q] = remote(
            cots.at[2 * q], cots.at[2 * q + 1], twin_ss.at[q], twin_rs.at[q], twin
        )
    pick_rows((3,))

    def pass_on(k):
        along[layers - k].wait_recv()
        block = window.at[(z + k) % layers, window_rows(c)]
        swap[k] = remote(block, block, wt_ss.at[k], wt_rs.at[k], twin)

    pass_on(1)
    slots = lax.broadcasted_iota(jnp.int32, (SLOTS, tokens), 0)

    def row_of(values, expert):
        return jnp.sum(jnp.where(names == expert, values, 0.0), axis=0, keepdims=True)

    shares = {}

    def make_share(q):
        if q:
            info[q].wait_recv()
            place_q, gate_q = info_got[q, 0], info_got[q, 1]
        else:
            place_q, gate_q = place, gate
        share = jnp.concatenate(
            [
                jnp.where(
                    slots == row_of(place_q, expert).astype(jnp.int32),
                    row_of(gate_q, expert),
                    0.0,
                )
                for expert in (e, peer(1))
            ],
            axis=0,
        )
        shares[q] = share.astype(jnp.bfloat16)
        rows[q].wait_recv()

    start = (chip * 2 * shard) // 128 * 128
    width = window.shape[1]

    def slab_of(k):
        return columns(((z + k) % layers) * slab, slab)

    def add_rows(q, k):
        here = slab_of(k)
        part[q, :, here] = lax.dot_general(
            shares[q], blocks[q, :, here], CONTRACT_FIRST, preferred_element_type=jnp.float32
        )

    def add_key(q, k):
        here = columns(((z + k) % layers) * slab + start, width)
        part[q, :, here] += lax.dot_general(
            cots[2 * q],
            window[(z + k) % layers],
            CONTRACT_LAST,
            preferred_element_type=jnp.float32,
        )

    to_x, to_y = (z, peer(2)), (z, peer(4))
    x_first = [(to_x, x_got), (to_y, y_got)]
    relays, direct, onward = {}, {}, {}

    def send_slab(q, k, dst, number, to):
        here = slab_of(k)
        return remote(
            send.at[q, :, here], dst.at[:, here], part_ss.at[number], part_rs.at[number], to
        )

    make_share(3)
    add_rows(3, 0)
    cot[3].wait_recv()
    cot[4].wait_recv()
    for k in range(layers):
        if k:
            add_rows(3, k)
        swap[k].wait_recv()
        add_key(3, k)
        here = slab_of(k)
        send[3, :, here] = part[3, :, here].astype(jnp.bfloat16)
        relays[k] = send_slab(3, k, relay_got, k, x_first[k % 2][0])
        if k == 1:
            pass_on(2)
            pass_on(3)

    for copy in [*forward.values(), *attn.values()]:
        copy.wait_recv()
    for across in range(2):
        near_cots = jnp.concatenate([cots[0:2], cots[2 + 2 * across : 4 + 2 * across]], axis=0)
        grad = lax.dot_general(
            attn_got[across].reshape(4 * tokens, layers * shard),
            near_cots.reshape(4 * tokens, keys),
            CONTRACT_FIRST,
            preferred_element_type=jnp.float32,
        ).reshape(layers, shard, keys)
        grad_own[:, across * shard : (across + 1) * shard, :] = grad
        grad_send[:, across * shard : (across + 1) * shard, :] = grad.astype(jnp.bfloat16)
    outward = {}
    for rz in (2, 1, 3):
        to = (z + rz) % layers
        outward[rz] = remote(
            grad_send.at[to], grad_got.at[rz], gz_ss.at[rz], gz_rs.at[rz], (to, e)
        )
    pick_rows((1, 2))
    make_share(1)
    make_share(2)
    for k in range(layers):
        q, (to, dst) = k % 2 + 1, x_first[k % 2]
        add_rows(q, k)
        add_key(q, k)
        here = slab_of(k)
        send[q, :, here] = part[q, :, here].astype(jnp.bfloat16)
        direct[k] = send_slab(q, k, dst, layers + k, to)
    for k in range(layers):
        q, (to, dst) = 2 - k % 2, x_first[1 - k % 2]
        add_rows(q, k)
        add_key(q, k)
        relays[k].wait_recv()
        here = slab_of(k)
        send[q, :, here] = (
            part[q, :, here] + relay_got[:, here].astype(jnp.float32)
        ).astype(jnp.bfloat16)
        onward[k] = send_slab(q, k, dst, 2 * layers + k, to)

    pick_rows((0,))
    inner = jnp.zeros((experts, tokens), jnp.float32)
    for r in range(experts):
        if r > 0:
            dots[r].wait_recv()
            got = dots_got[r, :, 0:SLOTS]
        else:
            got = dots_send[e, :, 0:SLOTS]
        expert = peer(r)
        hit = (slots == row_of(place, expert).astype(jnp.int32)).astype(jnp.float32)
        found = jnp.dot(
            got.astype(jnp.bfloat16),
            hit.astype(jnp.bfloat16),
            preferred_element_type=jnp.float32,
        )
        inner = inner + jnp.where(names == expert, found[0:1, :], 0.0)
    mean_inner = jnp.sum(gate * inner, axis=0, keepdims=True)
    d_probs = choose * (inner - mean_inner) / chosen_sum
    d_logits = probs * (d_probs - jnp.sum(probs * d_probs, axis=0, keepdims=True))
    d_parts = split_columns(d_logits)

    make_share(0)
    for k in range(layers):
        add_rows(0, k)
        add_key(0, k)

    loads[7].wait()

    def router_tile(i, _):
        here = columns(i * slab, slab)
        both = lax.dot_general(
            d_parts, router_ref[:, here], CONTRACT_FIRST, preferred_element_type=jnp.float32
        )
        part[0, :, here] += both[:tokens] + both[tokens:]
        return 0

    lax.fori_loop(0, layers, router_tile, 0)

    for rz in range(1, layers):
        outward[rz].wait_recv()
    grad_own[0] = (
        grad_own[z]
        + grad_got[1].astype(jnp.float32)
        + grad_got[2].astype(jnp.float32)
        + grad_got[3].astype(jnp.float32)
    )
    final = {}
    for across, mine_o, r in ((0, y, 4), (1, x, 2)):
        other = pl.ds(pl.multiple_of(across * shard + (1 - mine_o) * bit, 16), bit)
        cross_send[across] = grad_own[0, other, :].astype(jnp.bfloat16)
        final[across] = remote(
            cross_send.at[across],
            cross_got.at[across],
            gx_ss.at[across],
            gx_rs.at[across],
            (z, peer(r)),
        )
    for k in range(layers):
        direct[k].wait_recv()
        onward[k].wait_recv()
        here = slab_of(k)
        out_ref[:, here] = (
            part[0, :, here]
            + x_got[:, here].astype(jnp.float32)
            + y_got[:, here].astype(jnp.float32)
        ).astype(jnp.bfloat16)
    for across, mine_o in ((0, y), (1, x)):
        final[across].wait_recv()
        kept = pl.ds(pl.multiple_of(across * shard + mine_o * bit, 16), bit)
        grad_ref[across * bit : (across + 1) * bit, :] = grad_own[0, kept, :] + cross_got[
            across
        ].astype(jnp.float32)
    for group in (info, cot, attn, dots, rows, forward, outward, final):
        for copy in group.values():
            copy.wait_send()
    for group in (along, swap, relays, direct, onward):
        for copy in group.values():
            copy.wait_send()


def fused_local(
    attn_input,
    key_cot,
    routing,
    router_base,
    router_weight,
    expert_rows,
    expert_dots,
    key_weight,
    first_moment,
    second_moment,
):
    tokens, features = attn_input.shape
    experts, capacity, _ = expert_rows.shape
    shard, keys = key_weight.shape
    layers = lax.axis_size("dp")
    b16, f32 = jnp.bfloat16, jnp.float32
    vmem, anywhere = pl.BlockSpec(memory_space=pltpu.VMEM), pl.BlockSpec(memory_space=pl.ANY)
    dma = pltpu.SemaphoreType.DMA
    input_grad, key_grad = pl.pallas_call(
        fused,
        out_shape=(
            pltpu.VMEM((tokens, features), b16),
            pltpu.VMEM((shard, keys), f32),
        ),
        in_specs=[anywhere] * 8,
        out_specs=[vmem] * 2,
        scratch_shapes=[
            pltpu.VMEM((tokens, features), b16),
            pltpu.VMEM(routing.shape[::-1], jnp.int32),
            pltpu.VMEM(router_base.shape[::-1], f32),
            pltpu.VMEM(router_weight.shape[::-1], b16),
            pltpu.VMEM(expert_dots.shape, b16),
            pltpu.VMEM((shard, keys), f32),
            pltpu.VMEM((experts * capacity, features), b16),
            pltpu.VMEM((4, SLOTS, features), b16),
            pltpu.VMEM((4, 2 * SLOTS, features), b16),
            pltpu.VMEM((2, experts, tokens), f32),
            pltpu.VMEM((4, 2, experts, tokens), f32),
            pltpu.VMEM((experts, 8, 128), f32),
            pltpu.VMEM((experts, 8, 128), f32),
            pltpu.VMEM((experts, tokens, keys), b16),
            pltpu.VMEM((2, 4, tokens, layers * shard), b16),
            pltpu.VMEM((2, 4, tokens, layers * shard), b16),
            pltpu.VMEM((layers, 2 * shard + 64, keys), b16),
            pltpu.VMEM((4, tokens, features), f32),
            pltpu.VMEM((4, tokens, features), b16),
            pltpu.VMEM((tokens, features), b16),
            pltpu.VMEM((tokens, features), b16),
            pltpu.VMEM((tokens, features), b16),
            pltpu.VMEM((layers, 2 * shard, keys), f32),
            pltpu.VMEM((layers, 2 * shard, keys), b16),
            pltpu.VMEM((layers, 2 * shard, keys), b16),
            pltpu.VMEM((2, shard // 2, keys), b16),
            pltpu.VMEM((2, shard // 2, keys), b16),
            dma((8,)),
            dma((4,)),
            dma((4,)),
            dma((4,)),
            dma((4,)),
            dma((experts,)),
            dma((experts,)),
            dma((5,)),
            dma((5,)),
            dma((4,)),
            dma((4,)),
            dma((experts,)),
            dma((experts,)),
            dma((layers,)),
            dma((layers,)),
            dma((layers,)),
            dma((layers,)),
            dma((3 * layers,)),
            dma((3 * layers,)),
            dma((layers,)),
            dma((layers,)),
            dma((2,)),
            dma((2,)),
        ],
        compiler_params=pltpu.CompilerParams(
            collective_id=0, has_side_effects=True, vmem_limit_bytes=60 * 1024 * 1024
        ),
        cost_estimate=pl.CostEstimate(
            flops=6 * 10**9, bytes_accessed=10**7, transcendentals=10**4
        ),
    )(
        attn_input,
        key_cot,
        routing.T,
        router_base.T,
        router_weight.T,
        expert_rows.transpose(1, 0, 2).reshape(capacity * experts, features),
        expert_dots,
        key_weight,
    )
    return (input_grad, *adamw(key_weight, first_moment, second_moment, key_grad))


def solution(mesh):
    fits = mesh.shape["dp"] == 4 and mesh.shape["expert"] == 8
    in_specs = (
        P(("dp", "expert"), None),
        P(("dp", "expert"), None),
        P(("dp", "expert"), None),
        P(("dp", "expert"), None),
        P(),
        P(("dp", "expert"), None, None),
        P(("dp", "expert"), None),
        P(("dp", "expert"), None),
        P(("dp", "expert"), None),
        P(("dp", "expert"), None),
    )
    out_specs = (
        P(("dp", "expert"), None),
        P(("dp", "expert"), None),
        P(("dp", "expert"), None),
        P(("dp", "expert"), None),
    )
    return jax.shard_map(
        fused_local if fits else local, mesh=mesh, in_specs=in_specs, out_specs=out_specs, check_vma=False)
```
